32 devices in a mesh: ctx: 8 (over z, x), dp: 4 (over y, core).
Axes of the slice: x: 2, y: 2, z: 4, core: 2. Of those that a mesh axis runs over, the one named last changes fastest.
Arguments:
- queries: bfloat16 [4, 1024, 512], P('dp', 'ctx'), may hold values from -6 to 6
- keys: bfloat16 [4, 1024, 512], P('dp', 'ctx'), may hold values from -6 to 6
- values: bfloat16 [4, 1024, 512], P('dp', 'ctx'), may hold values from -6 to 6
- global_keys: bfloat16 [128, 512], replicated, may hold values from -6 to 6
- global_values: bfloat16 [128, 512], replicated, may hold values from -6 to 6
- upstream: bfloat16 [4, 1024, 512], P('dp', 'ctx'), may hold values from -6 to 6
- partner_shard: int32 [16, 3], replicated, may hold values from 0 to 7, as said below
- partner_block: int32 [16, 3], replicated, may hold values from 0 to 1
Outputs:
- attention: bfloat16 [4, 1024, 512], P('dp', 'ctx')
- grad_queries: bfloat16 [4, 1024, 512], P('dp', 'ctx')
- grad_keys: bfloat16 [4, 1024, 512], P('dp', 'ctx')
- grad_values: bfloat16 [4, 1024, 512], P('dp', 'ctx')
- grad_global_keys: float32 [128, 512], replicated
- grad_global_values: float32 [128, 512], replicated
The draws below stay inside these ranges and needn't reach their ends.
Inputs may be any that keep to these rules, and one draw needn't show every extreme that they name: `partner_shard`: row i describes query block i of every sequence, which lies on shard i // 2. Each entry differs from i // 2 in exactly one bit of the shard index. For every shard and every bit, at most 2 of the shard's 2 * 3 entries use that bit, and on every shard some bit is used by exactly 2 of them.
All inputs are finite; a program needn't handle non-finite values.
Results may differ from the reference program's by a relative error of at most 0.0076.
Values may be sent and summed in bfloat16 or wider, within the bound.
A program may use at most 64 MiB of HBM per device.

```python
import math
import jax
import jax.numpy as jnp
from jax import lax

HEAD_DIM = 64
BLOCK = 64
R = 3
G = 128
DA = 512
NBD = 2
SEQ = 1024
BATCH = 4
NBLK = 16
BITS = 3
CAP = 2
N_CTX = 8


def draw_queries(key, part):
    base = jnp.clip(jax.random.normal(jax.random.fold_in(key, 1), (BATCH, SEQ, DA), jnp.float32), -6.0, 6.0)
    return base.astype(jnp.bfloat16)


def draw_global_keys(key, part):
    base = jnp.clip(jax.random.normal(jax.random.fold_in(key, 3), (G, DA), jnp.float32), -6.0, 6.0)
    return base.astype(jnp.bfloat16)


def deal_bits(sub_key):
    requests = NBD * R
    first_key, second_key = jax.random.split(sub_key)
    bit_pool = jnp.repeat(jnp.arange(BITS, dtype=jnp.int32), CAP)
    shuffled = jax.random.permutation(first_key, bit_pool)
    doubled = shuffled[0]
    sort_keys = jnp.where(shuffled == doubled, 0, 1).astype(jnp.int32)
    order = jnp.argsort(sort_keys, stable=True)
    dealt = shuffled[order][:requests]
    return jax.random.permutation(second_key, dealt)


def draw_partner_shard(key, part):
    shard_total = NBLK // NBD
    shard_ids = jnp.arange(shard_total, dtype=jnp.int32)
    sub_keys = jax.random.split(jax.random.fold_in(key, 11), shard_total)
    dealt_bits = jax.vmap(deal_bits)(sub_keys)
    stride = jnp.power(2, dealt_bits).astype(jnp.int32)
    bit_set = shard_ids[:, None] // stride % 2
    partner = shard_ids[:, None] + stride * (1 - 2 * bit_set)
    return partner.reshape(NBLK, R).astype(jnp.int32)


def with_ends(result, rng, smallest, high):
    longest = result.shape.index(max(result.shape))
    spots = []
    for shift in (0, 1):
        where = [jax.random.randint(jax.random.fold_in(rng, axis), (), 0, length) for axis, length in enumerate(result.shape)]
        where[longest] = (where[longest] + shift) % result.shape[longest]
        spots.append(tuple(where))
    return result.at[spots[0]].set(smallest).at[spots[1]].set(high)


def shard_levels(stream_key, dims, pieces, smallest, top_value):
    loudness, own = 1.0, jax.random.fold_in(stream_key, 6)
    for position, parts in pieces:
        heights = jnp.exp(jax.random.uniform(jax.random.fold_in(own, position), (parts,), jnp.float32, smallest / len(pieces), top_value / len(pieces)))
        loudness = loudness * jnp.repeat(heights, dims[position] // parts).reshape([-1 if axis == position else 1 for axis in range(len(dims))])
    return loudness


def scatter_about(rng, extent, deviation, bound, cuts=(), held_as=jnp.bfloat16):
    array = jax.random.normal(rng, extent, jnp.float32) * deviation
    if len(cuts) > 0:
        array = shard_levels(rng, extent, cuts, -0.22, 0.18) * array
    return jnp.clip(array, min=-bound, max=bound).astype(held_as)


def setup_inputs(seed: int = 0) -> dict:
    streams_of = jax.random.split(jax.random.key(seed), 9)
    return {
        "queries": draw_queries(jax.random.fold_in(streams_of[8], 71), 0),
        "keys": scatter_about(streams_of[1], (BATCH, SEQ, DA), 1.0, 6.0, ((0, 4), (1, 8))),
        "values": scatter_about(streams_of[2], (BATCH, SEQ, DA), 1.0, 6.0, ((0, 4), (1, 8))),
        "global_keys": draw_global_keys(jax.random.fold_in(streams_of[8], 71), 0),
        "global_values": scatter_about(streams_of[4], (G, DA), 1.0, 6.0),
        "upstream": scatter_about(streams_of[5], (BATCH, SEQ, DA), 1.0, 6.0, ((0, 4), (1, 8))),
        "partner_shard": draw_partner_shard(jax.random.fold_in(streams_of[8], 71), 0),
        "partner_block": with_ends(jax.random.randint(streams_of[7], (NBLK, R), 0, NBD), jax.random.fold_in(streams_of[7], 1), 0, NBD - 1).astype(jnp.int32),
    }


masked_score = -1e+30

def to_low(values_in):
    return lax.optimization_barrier(values_in.astype(jnp.bfloat16))

def valid_keys_for(block_ids, total_blocks, global_count):
    block_count = block_ids.shape[0]
    left_open = jnp.broadcast_to((block_ids > 0)[:, None], (block_count, BLOCK))
    right_open = jnp.broadcast_to((block_ids < total_blocks - 1)[:, None], (block_count, BLOCK))
    center = jnp.ones((block_count, BLOCK), jnp.bool_)
    remote = jnp.ones((block_count, R * BLOCK + global_count), jnp.bool_)
    return jnp.concatenate([left_open, center, right_open, remote], axis=1)

def block_terms(query_blocks, upstream_blocks, key_rows, valid_keys):
    block_count = query_blocks.shape[0]
    full_width = query_blocks.shape[2]
    head_count = full_width // HEAD_DIM
    key_count = key_rows.shape[1]
    scaling = 1.0 / math.sqrt(HEAD_DIM)
    query_heads = query_blocks.astype(jnp.float32).reshape(block_count, BLOCK, head_count, HEAD_DIM)
    grad_heads = upstream_blocks.astype(jnp.float32).reshape(block_count, BLOCK, head_count, HEAD_DIM)
    key_heads = key_rows[:, :, :full_width].astype(jnp.float32).reshape(block_count, key_count, head_count, HEAD_DIM)
    value_heads = key_rows[:, :, full_width:].astype(jnp.float32).reshape(block_count, key_count, head_count, HEAD_DIM)
    scores = jnp.einsum('nqhd,nkhd->nhqk', query_heads, key_heads) * scaling
    scores = jnp.where(valid_keys[:, None, None, :], scores, masked_score)
    row_max = lax.optimization_barrier(jnp.max(scores, axis=3, keepdims=True))
    weights = jnp.exp(scores - row_max)
    probs_full = weights / lax.optimization_barrier(jnp.sum(weights, axis=3, keepdims=True))
    probs_low = to_low(probs_full).astype(jnp.float32)
    attention = jnp.einsum('nhqk,nkhd->nqhd', probs_low, value_heads)
    grad_probs = jnp.einsum('nqhd,nkhd->nhqk', grad_heads, value_heads)
    inner_sum = lax.optimization_barrier(jnp.sum(probs_full * grad_probs, axis=3, keepdims=True))
    grad_scores = to_low(probs_full * (grad_probs - inner_sum) * scaling).astype(jnp.float32)
    grad_query = jnp.einsum('nhqk,nkhd->nqhd', grad_scores, key_heads)
    key_terms = jnp.einsum('nhqk,nqhd->nkhd', grad_scores, query_heads).reshape(block_count, key_count, full_width)
    value_terms = jnp.einsum('nhqk,nqhd->nkhd', probs_low, grad_heads).reshape(block_count, key_count, full_width)
    all_terms = jnp.concatenate([key_terms, value_terms], axis=2)
    attention = attention.reshape(block_count, BLOCK, full_width).astype(jnp.bfloat16)
    grad_query = grad_query.reshape(block_count, BLOCK, full_width).astype(jnp.bfloat16)
    return (attention, grad_query, all_terms)

def reference(queries, keys, values, global_keys, global_values, upstream, partner_shard, partner_block):
    full_width = queries.shape[2]
    pair_width = 2 * full_width
    global_pairs = jnp.concatenate([global_keys, global_values], axis=1)
    global_count = global_pairs.shape[0]
    targets = (partner_shard * NBD + partner_block).astype(jnp.int32)

    def one_sequence(seq_args):
        query_seq, key_seq, value_seq, upstream_seq = seq_args
        pair_blocks = jnp.concatenate([key_seq, value_seq], axis=1).reshape(NBLK, BLOCK, pair_width)
        padded = jnp.pad(pair_blocks, ((1, 1), (0, 0), (0, 0)))
        query_shards = query_seq.reshape(N_CTX, NBD, BLOCK, full_width)
        upstream_shards = upstream_seq.reshape(N_CTX, NBD, BLOCK, full_width)

        def one_shard(shard_args):
            shard_index, query_blocks, upstream_blocks = shard_args
            first_block = (shard_index * NBD).astype(jnp.int32)
            window = lax.dynamic_slice_in_dim(padded, first_block, NBD + 2, 0)
            window_rows = jnp.concatenate([window[0:NBD], window[1:NBD + 1], window[2:NBD + 2]], axis=1)
            own_targets = lax.dynamic_slice_in_dim(targets, first_block, NBD, 0).reshape(NBD * R)
            random_rows = jnp.take(pair_blocks, own_targets, axis=0).reshape(NBD, R * BLOCK, pair_width)
            shared = jnp.broadcast_to(global_pairs[None], (NBD, global_count, pair_width))
            key_rows = jnp.concatenate([window_rows, random_rows, shared], axis=1)
            block_ids = first_block + jnp.arange(NBD, dtype=jnp.int32)
            valid_keys = valid_keys_for(block_ids, NBLK, global_count)
            attention, grad_query, all_terms = block_terms(query_blocks, upstream_blocks, key_rows, valid_keys)
            window_terms = all_terms[:, :3 * BLOCK].reshape(NBD, 3, BLOCK, pair_width)
            placed = jnp.pad(window_terms[:, 0], ((0, 2), (0, 0), (0, 0))) + jnp.pad(window_terms[:, 1], ((1, 1), (0, 0), (0, 0))) + jnp.pad(window_terms[:, 2], ((2, 0), (0, 0), (0, 0)))
            random_terms = to_low(all_terms[:, 3 * BLOCK:(3 + R) * BLOCK]).reshape(NBD * R, BLOCK, pair_width)
            global_terms = lax.optimization_barrier(jnp.sum(all_terms[:, (3 + R) * BLOCK:], axis=0))
            return (attention, grad_query, placed[1:NBD + 1], to_low(placed[0]), to_low(placed[NBD + 1]), random_terms, global_terms)
        results = lax.map(one_shard, (jnp.arange(N_CTX, dtype=jnp.int32), query_shards, upstream_shards))
        attention, grad_query, local_grads, to_left, to_right, random_terms, global_terms = results
        zero_block = jnp.zeros((1, BLOCK, pair_width), jnp.float32)
        from_left = jnp.concatenate([zero_block, to_right[:-1].astype(jnp.float32)], axis=0)
        from_right = jnp.concatenate([to_left[1:].astype(jnp.float32), zero_block], axis=0)
        local_grads = local_grads.at[:, 0].add(from_left)
        local_grads = local_grads.at[:, NBD - 1].add(from_right)
        flat_grads = local_grads.reshape(NBLK, BLOCK, pair_width)
        flat_grads = flat_grads.at[targets.reshape(NBLK * R)].add(random_terms.reshape(NBLK * R, BLOCK, pair_width).astype(jnp.float32))
        grad_pairs = flat_grads.reshape(SEQ, pair_width)
        return (attention.reshape(SEQ, full_width), grad_query.reshape(SEQ, full_width), grad_pairs[:, :full_width].astype(jnp.bfloat16), grad_pairs[:, full_width:].astype(jnp.bfloat16), lax.optimization_barrier(jnp.sum(global_terms, axis=0)))
    outputs = lax.map(one_sequence, (queries, keys, values, upstream))
    attention, grad_queries, grad_keys, grad_values, global_sums = outputs
    global_total = lax.optimization_barrier(jnp.sum(global_sums, axis=0))
    return (attention, grad_queries, grad_keys, grad_values, global_total[:, :full_width], global_total[:, full_width:])
```

```python
import functools
import math

import jax
import jax.numpy as jnp
from jax import lax
from jax.experimental import pallas as pl
from jax.experimental.pallas import tpu as pltpu
from jax.sharding import PartitionSpec as P

HEAD_DIM = 64
BLOCK = 64
R = 3
LANES = 128
MASKED = -1e30
MESH = pl.DeviceIdType.MESH
NT = (((1,), (1,)), ((), ()))
TN = (((0,), (0,)), ((), ()))


def reduce_stages(sizes, rows):
    stages = []
    for axis, size in sizes:
        stride = 1
        while stride < size:
            radix = min(8, size // stride)
            if rows % (radix * 16) == 0:
                rows //= radix
            stages.append((axis, stride, radix, rows))
            stride *= radix
    return stages


def kernel(
    shards, stages, q_ref, k_ref, v_ref, gk_ref, gv_ref, u_ref, ps_ref, pb_ref,
    att_ref, dq_ref, dk_ref, dv_ref, dgk_ref, dgv_ref,
    kv, bias, terms, back, own, *rest,
):
    count = len(stages)
    accs, recvs = rest[:count], rest[count : 2 * count]
    final = rest[2 * count]
    kv_send, kv_recv, t_send, t_recv = rest[2 * count + 1 : 2 * count + 5]
    sems = rest[2 * count + 5 :]
    rs_send, rs_recv = sems[:count], sems[count : 2 * count]
    ag_send, ag_recv = sems[2 * count : 3 * count], sems[3 * count :]

    rows, width = q_ref.shape
    blocks = rows // BLOCK
    chunks = width // LANES
    bits = shards.bit_length() - 1
    globals_ = gk_ref.shape[0]
    edge_at = rows * (1 + bits)
    glob_at = edge_at + BLOCK
    total = kv.shape[2]
    me = lax.axis_index("ctx")
    spot = {"ctx": me, "dp": lax.axis_index("dp")}
    odd = lax.rem(me, 2)
    edge_peer = me - 1 + 2 * odd
    has_edge = jnp.logical_and(edge_peer >= 0, edge_peer < shards)
    edge_first = pl.multiple_of(odd * (rows - BLOCK), BLOCK)
    peers = [me + (1 << b) * (1 - 2 * lax.rem(lax.div(me, 1 << b), 2)) for b in range(bits)]

    barrier = pltpu.get_barrier_semaphore()

    def greet(axis, to):
        pl.semaphore_signal(barrier, inc=1, device_id={axis: to}, device_id_type=MESH)

    greeted = 0
    for axis, stride, radix, _ in stages:
        digit = lax.rem(lax.div(spot[axis], stride), radix)
        for k in range(1, radix):
            greet(axis, spot[axis] + (lax.rem(digit + k, radix) - digit) * stride)
            greeted += 1

    apart = all(radix < shards for axis, _, radix, _ in stages if axis == "ctx")
    if apart:

        @pl.when(has_edge)
        def _():
            greet("ctx", edge_peer)

    for c in range(chunks):
        lanes = slice(c * LANES, (c + 1) * LANES)
        kv[c, 0, 0:rows] = k_ref[:, lanes]
        kv[c, 1, 0:rows] = v_ref[:, lanes]

    pl.semaphore_wait(barrier, greeted + jnp.where(has_edge, 1, 0) if apart else greeted)

    def kv_copy(c, b):
        return pltpu.make_async_remote_copy(
            src_ref=kv.at[c, :, pl.ds(0, rows)],
            dst_ref=kv.at[c, :, pl.ds(rows * (1 + b), rows)],
            send_sem=kv_send.at[c, b], recv_sem=kv_recv.at[c, b],
            device_id={"ctx": peers[b]}, device_id_type=MESH,
        )

    def kv_edge(c):
        return pltpu.make_async_remote_copy(
            src_ref=kv.at[c, :, pl.ds(edge_first, BLOCK)],
            dst_ref=kv.at[c, :, pl.ds(edge_at, BLOCK)],
            send_sem=kv_send.at[c, bits], recv_sem=kv_recv.at[c, bits],
            device_id={"ctx": edge_peer}, device_id_type=MESH,
        )

    def term_copy(c, b):
        return pltpu.make_async_remote_copy(
            src_ref=terms.at[c, :, pl.ds(rows * b, rows)],
            dst_ref=back.at[c, :, pl.ds(rows * b, rows)],
            send_sem=t_send.at[c, b], recv_sem=t_recv.at[c, b],
            device_id={"ctx": peers[b]}, device_id_type=MESH,
        )

    def term_edge(c):
        return pltpu.make_async_remote_copy(
            src_ref=terms.at[c, :, pl.ds(rows * bits, BLOCK)],
            dst_ref=back.at[c, :, pl.ds(rows * bits, BLOCK)],
            send_sem=t_send.at[c, bits], recv_sem=t_recv.at[c, bits],
            device_id={"ctx": edge_peer}, device_id_type=MESH,
        )

    order = list(range(bits))[::-1]
    for c in range(chunks):
        for b in order:
            kv_copy(c, b).start()

        @pl.when(has_edge)
        def _():
            kv_edge(c).start()

    for c in range(chunks):
        lanes = slice(c * LANES, (c + 1) * LANES)
        kv[c, 0, glob_at : glob_at + globals_] = gk_ref[:, lanes]
        kv[c, 1, glob_at : glob_at + globals_] = gv_ref[:, lanes]
        if total > glob_at + globals_:
            kv[c, :, glob_at + globals_ :] = jnp.zeros(
                (2, total - glob_at - globals_, LANES), kv.dtype
            )

    @pl.when(jnp.logical_not(has_edge))
    def _():
        kv[:, :, edge_at : edge_at + BLOCK] = jnp.zeros((chunks, 2, BLOCK, LANES), kv.dtype)
        back[:, :, rows * bits : rows * bits + BLOCK] = jnp.zeros(
            (chunks, 2, BLOCK, LANES), back.dtype
        )

    pair = 2 * rows
    query_block = lax.rem(lax.div(lax.broadcasted_iota(jnp.int32, (8, pair), 1), BLOCK), blocks)
    first_block = me * blocks
    listed = [
        [(ps_ref[first_block + n, r], pb_ref[first_block + n, r]) for r in range(R)]
        for n in range(blocks)
    ]

    def put_bias(at, counts):
        times = jnp.zeros((8, pair), jnp.int32)
        for n in range(blocks):
            times = jnp.where(query_block == n, counts[n], times)
        times = times.astype(jnp.float32)
        line = jnp.where(times > 0.5, jnp.log(jnp.maximum(times, 1.0)), MASKED)
        for step in range(BLOCK // 8):
            bias[at + step * 8 : at + step * 8 + 8] = line

    for j in range(blocks):
        put_bias(j * BLOCK, [jnp.int32(1 if abs(j - n) <= 1 else 0) for n in range(blocks)])
    for b in range(bits):
        for j in range(blocks):
            counts = []
            for n in range(blocks):
                times = jnp.int32(0)
                for shard, block in listed[n]:
                    times += jnp.where(shard == peers[b], 1, 0) * jnp.where(block == j, 1, 0)
                if b == 0 and j == 0 and n == blocks - 1:
                    times += 1 - odd
                if b == 0 and j == blocks - 1 and n == 0:
                    times += odd
                counts.append(times)
            put_bias(rows * (1 + b) + j * BLOCK, counts)
    valid = jnp.where(has_edge, 1, 0)
    edge_counts = [jnp.int32(0)] * blocks
    edge_counts[0] = edge_counts[0] + (1 - odd) * valid
    edge_counts[blocks - 1] = edge_counts[blocks - 1] + odd * valid
    put_bias(edge_at, edge_counts)
    for at in range(glob_at, glob_at + globals_, BLOCK):
        put_bias(at, [jnp.int32(1)] * blocks)
    if total > glob_at + globals_:
        bias[glob_at + globals_ :] = jnp.full((total - glob_at - globals_, pair), MASKED)

    low_head = lax.broadcasted_iota(jnp.int32, (rows, LANES), 1) < HEAD_DIM
    scaling = 1.0 / math.sqrt(HEAD_DIM)

    def both_heads(x):
        x = x.astype(jnp.float32)
        zero = jnp.zeros_like(x)
        return jnp.concatenate(
            [jnp.where(low_head, x, zero), jnp.where(low_head, zero, x)], axis=0
        )

    def dot(a, b, dims):
        return lax.dot_general(a, b, dims, preferred_element_type=jnp.float32)

    NN = (((1,), (0,)), ((), ()))

    def step(c, carry):
        lanes = pl.ds(pl.multiple_of(c * LANES, LANES), LANES)
        queries = (both_heads(q_ref[:, lanes]) * scaling).astype(jnp.bfloat16)
        grads = both_heads(u_ref[:, lanes]).astype(jnp.bfloat16)
        for b in order:
            kv_copy(c, b).wait_recv()

        @pl.when(has_edge)
        def _():
            kv_edge(c).wait_recv()

        keys = kv[c, 0]
        values = kv[c, 1]
        scores = dot(keys, queries, NT) + bias[...]
        weights = jnp.exp(scores - jnp.max(scores, axis=0, keepdims=True))
        probs = weights * (1.0 / jnp.sum(weights, axis=0, keepdims=True))
        low = probs.astype(jnp.bfloat16)
        dprobs = dot(values, grads, NT)
        inner = jnp.sum(probs * dprobs, axis=0, keepdims=True)
        dscores = (probs * (dprobs - inner)).astype(jnp.bfloat16)
        for which, (left, right) in enumerate(((dscores, queries), (low, grads))):
            made = dot(left, right, NN)
            own[c, which] = made[0:rows]
            terms[c, which] = made[rows:glob_at].astype(jnp.bfloat16)
            accs[0][
                pl.ds(pl.multiple_of((c * 2 + which) * globals_, globals_), globals_)
            ] = made[glob_at : glob_at + globals_].astype(jnp.bfloat16)
        for b in order:
            term_copy(c, b).start()

        @pl.when(has_edge)
        def _():
            term_edge(c).start()

        attention = dot(low, values, TN)
        att_ref[:, lanes] = jnp.where(low_head, attention[:rows], attention[rows:]).astype(
            jnp.bfloat16
        )
        dqueries = dot(dscores, keys, TN)
        dq_ref[:, lanes] = (
            jnp.where(low_head, dqueries[:rows], dqueries[rows:]) * scaling
        ).astype(jnp.bfloat16)
        return carry

    lax.fori_loop(0, chunks, step, 0)

    def digit_of(i):
        axis, stride, radix, _ = stages[i]
        return lax.rem(lax.div(spot[axis], stride), radix)

    def peer_of(i, k):
        axis, stride, radix, _ = stages[i]
        digit = digit_of(i)
        other = lax.rem(digit + k, radix)
        return other, {axis: spot[axis] + (other - digit) * stride}

    def scatter_copy(i, k):
        held = stages[i][3]
        other, device = peer_of(i, k)
        at = other * held if accs[i].shape[0] != held else 0
        return pltpu.make_async_remote_copy(
            src_ref=accs[i].at[pl.ds(pl.multiple_of(at, 16), held)],
            dst_ref=recvs[i].at[k - 1],
            send_sem=rs_send[i].at[k - 1], recv_sem=rs_recv[i].at[k - 1],
            device_id=device, device_id_type=MESH,
        )

    starts = []
    start = 0
    for i, (axis, stride, radix, held) in enumerate(stages):
        if accs[i].shape[0] != held:
            start = start + digit_of(i) * held
        starts.append(start)

    def scatter_start(i):
        for k in range(1, stages[i][2]):
            scatter_copy(i, k).start()

    def scatter_end(i):
        held = stages[i][3]
        at = digit_of(i) * held if accs[i].shape[0] != held else 0
        summed = accs[i][pl.ds(pl.multiple_of(at, 16), held)].astype(jnp.float32)
        for k in range(1, stages[i][2]):
            scatter_copy(i, k).wait_recv()
            summed = summed + recvs[i][k - 1].astype(jnp.float32)
        summed = summed.astype(jnp.bfloat16)
        if i + 1 < count:
            accs[i + 1][...] = summed
        else:
            final[pl.ds(pl.multiple_of(starts[i], 16), held)] = summed

    def gather_copy(i, k, at):
        held = stages[i][3]
        part = final.at[pl.ds(pl.multiple_of(at, 16), held)]
        return pltpu.make_async_remote_copy(
            src_ref=part, dst_ref=part,
            send_sem=ag_send[i].at[k - 1], recv_sem=ag_recv[i].at[k - 1],
            device_id=peer_of(i, k)[1], device_id_type=MESH,
        )

    def gather_start(i):
        for k in range(1, stages[i][2]):
            gather_copy(i, k, starts[i]).start()

    def gather_end(i):
        _, _, radix, held = stages[i]
        for k in range(1, radix):
            behind = lax.rem(digit_of(i) + radix - k, radix)
            gather_copy(i, k, starts[i] + (behind - digit_of(i)) * held).wait_recv()

    def collect(c):
        lanes = slice(c * LANES, (c + 1) * LANES)
        for b in order:
            term_copy(c, b).wait_recv()

        @pl.when(has_edge)
        def _():
            term_edge(c).wait_recv()

        low_rows = lax.broadcasted_iota(jnp.int32, (rows, LANES), 0)
        at_edge = jnp.logical_and(low_rows >= edge_first, low_rows < edge_first + BLOCK)
        for which, out in enumerate((dk_ref, dv_ref)):
            summed = own[c, which]
            for b in range(bits):
                summed = summed + back[c, which, rows * b : rows * (b + 1)].astype(jnp.float32)
            edge = back[c, which, rows * bits : rows * bits + BLOCK].astype(jnp.float32)
            edge = jnp.concatenate([edge] * blocks, axis=0)
            summed = summed + jnp.where(at_edge, edge, 0.0)
            out[:, lanes] = summed.astype(jnp.bfloat16)

    for i in range(count):
        scatter_start(i)
        scatter_end(i)
    split = [i for i in range(count) if accs[i].shape[0] != stages[i][3]]
    todo = list(range(chunks))
    for i in split[::-1]:
        gather_start(i)
        if todo:
            collect(todo.pop(0))
        gather_end(i)
    for c in range(chunks):
        lanes = slice(c * LANES, (c + 1) * LANES)
        for which, out in enumerate((dgk_ref, dgv_ref)):
            at = (c * 2 + which) * globals_
            out[:, lanes] = final[at : at + globals_].astype(jnp.float32)
    for c in todo:
        collect(c)

    for c in range(chunks):
        for b in order:
            kv_copy(c, b).wait_send()
            term_copy(c, b).wait_send()

        @pl.when(has_edge)
        def _():
            kv_edge(c).wait_send()
            term_edge(c).wait_send()

    for i in range(count):
        for k in range(1, stages[i][2]):
            scatter_copy(i, k).wait_send()
            if i in split:
                gather_copy(i, k, starts[i]).wait_send()


def body(shards, replicas, queries, keys, values, global_keys, global_values, upstream, ps, pb):
    _, rows, width = queries.shape
    globals_ = global_keys.shape[0]
    bits = shards.bit_length() - 1
    chunks = width // LANES
    used = rows * (1 + bits) + BLOCK + globals_
    total = -(-used // LANES) * LANES
    gathered = 2 * chunks * globals_
    stages = reduce_stages((("dp", replicas), ("ctx", shards)), gathered)
    low = jnp.bfloat16
    accs, recvs, sems = [], [], []
    held = gathered
    for _, _, radix, after in stages:
        accs.append(pltpu.VMEM((held, LANES), low))
        recvs.append(pltpu.VMEM((radix - 1, after, LANES), low))
        sems.append(pltpu.SemaphoreType.DMA((radix - 1,)))
        held = after
    vmem = pl.BlockSpec(memory_space=pltpu.VMEM)
    smem = pl.BlockSpec(memory_space=pltpu.SMEM)
    dma = pltpu.SemaphoreType.DMA((chunks, bits + 1))
    remote = rows * bits + BLOCK
    outs = pl.pallas_call(
        functools.partial(kernel, shards, stages),
        out_shape=[jax.ShapeDtypeStruct((rows, width), low)] * 4
        + [jax.ShapeDtypeStruct((globals_, width), jnp.float32)] * 2,
        in_specs=[vmem] * 6 + [smem] * 2,
        out_specs=[vmem] * 6,
        scratch_shapes=[
            pltpu.VMEM((chunks, 2, total, LANES), low),
            pltpu.VMEM((total, 2 * rows), jnp.float32),
            pltpu.VMEM((chunks, 2, remote, LANES), low),
            pltpu.VMEM((chunks, 2, remote, LANES), low),
            pltpu.VMEM((chunks, 2, rows, LANES), jnp.float32),
            *accs,
            *recvs,
            pltpu.VMEM((gathered, LANES), low),
            dma, dma, dma, dma,
            *sems, *sems, *sems, *sems,
        ],
        compiler_params=pltpu.CompilerParams(
            collective_id=0, has_side_effects=True, vmem_limit_bytes=40 * 1024 * 1024
        ),
    )(queries[0], keys[0], values[0], global_keys, global_values, upstream[0], ps, pb)
    return (outs[0][None], outs[1][None], outs[2][None], outs[3][None], outs[4], outs[5])


def solution(mesh):
    split = P("dp", "ctx", None)
    return jax.shard_map(
        functools.partial(body, mesh.shape["ctx"], mesh.shape["dp"]),
        mesh=mesh,
        in_specs=(split, split, split, P(), P(), split, P(), P()),
        out_specs=(split, split, split, split, P(), P()),
        check_vma=False,
    )
```

```python
import functools
import math

import jax
import jax.numpy as jnp
from jax import lax
from jax.experimental import pallas as pl
from jax.experimental.pallas import tpu as pltpu
from jax.sharding import PartitionSpec as P

HEAD_DIM = 64
BLOCK = 64
R = 3
LANES = 128
VMEM_BYTES = 63 * 1024 * 1024
MASKED = -1e30
MESH = pl.DeviceIdType.MESH
NT = (((1,), (1,)), ((), ()))
TN = (((0,), (0,)), ((), ()))


def reduce_stages(sizes, rows):
    stages = []
    for axis, size in sizes:
        stride = 1
        while stride < size:
            radix = min(8, size // stride)
            if rows % (radix * 16) == 0:
                rows //= radix
            stages.append((axis, stride, radix, rows))
            stride *= radix
    return stages


def kernel(
    shards, stages, q_hbm, k_hbm, v_hbm, gk_hbm, gv_hbm, u_hbm, ps_hbm, pb_hbm,
    *refs,
):
    outs_hbm, (att_ref, dq_ref, dk_ref, dv_ref, dgk_ref, dgv_ref) = refs[:6], refs[6:12]
    run(
        shards, stages, q_hbm, k_hbm, v_hbm, gk_hbm, gv_hbm, u_hbm, ps_hbm, pb_hbm, outs_hbm,
        att_ref, dq_ref, dk_ref, dv_ref, dgk_ref, dgv_ref, *refs[12:],
    )


def run(
    shards, stages, q_hbm, k_hbm, v_hbm, gk_hbm, gv_hbm, u_hbm, ps_hbm, pb_hbm, outs_hbm,
    att_ref, dq_ref, dk_ref, dv_ref, dgk_ref, dgv_ref, out_sem,
    q_ref, u_ref, ps_ref, pb_ref, in_sem, own_sem, kv, bias, terms, back, own, *rest,
):
    count = len(stages)
    accs, recvs = rest[:count], rest[count : 2 * count]
    final = rest[2 * count]
    kv_send, kv_recv, t_send, t_recv = rest[2 * count + 1 : 2 * count + 5]
    sems = rest[2 * count + 5 :]
    rs_send, rs_recv = sems[:count], sems[count : 2 * count]
    ag_send, ag_recv = sems[2 * count : 3 * count], sems[3 * count :]

    rows, width = q_hbm.shape
    blocks = rows // BLOCK
    chunks = width // LANES
    bits = shards.bit_length() - 1
    globals_ = gk_hbm.shape[0]
    edge_at = rows * (1 + bits)
    glob_at = edge_at + BLOCK
    total = kv.shape[2]
    me = lax.axis_index("ctx")
    spot = {"ctx": me, "dp": lax.axis_index("dp")}
    odd = lax.rem(me, 2)
    edge_peer = me - 1 + 2 * odd
    has_edge = jnp.logical_and(edge_peer >= 0, edge_peer < shards)
    edge_first = pl.multiple_of(odd * (rows - BLOCK), BLOCK)
    peers = [me + (1 << b) * (1 - 2 * lax.rem(lax.div(me, 1 << b), 2)) for b in range(bits)]

    barrier = pltpu.get_barrier_semaphore()

    def greet(axis, to):
        pl.semaphore_signal(barrier, inc=1, device_id={axis: to}, device_id_type=MESH)

    greeted = 0
    for axis, stride, radix, _ in stages:
        digit = lax.rem(lax.div(spot[axis], stride), radix)
        for k in range(1, radix):
            greet(axis, spot[axis] + (lax.rem(digit + k, radix) - digit) * stride)
            greeted += 1

    apart = all(radix < shards for axis, _, radix, _ in stages if axis == "ctx")
    if apart:

        @pl.when(has_edge)
        def _():
            greet("ctx", edge_peer)

    own_copies, in_copies = [], []
    for c in range(chunks):
        lanes = pl.ds(c * LANES, LANES)
        for which, (part, shared) in enumerate(((k_hbm, gk_hbm), (v_hbm, gv_hbm))):
            own_copies.append(
                pltpu.make_async_copy(
                    part.at[:, lanes], kv.at[c, which, pl.ds(0, rows)], own_sem.at[0, c, which]
                )
            )
            in_copies.append(
                pltpu.make_async_copy(
                    shared.at[:, lanes],
                    kv.at[c, which, pl.ds(glob_at, globals_)],
                    own_sem.at[1, c, which],
                )
            )
    for i, (src, dst) in enumerate(
        ((ps_hbm, ps_ref), (pb_hbm, pb_ref), (q_hbm, q_ref), (u_hbm, u_ref))
    ):
        in_copies.append(pltpu.make_async_copy(src, dst, in_sem.at[i]))
    for copy in own_copies + in_copies:
        copy.start()
    for copy in own_copies:
        copy.wait()

    pl.semaphore_wait(barrier, greeted + jnp.where(has_edge, 1, 0) if apart else greeted)

    def kv_copy(c, b):
        return pltpu.make_async_remote_copy(
            src_ref=kv.at[c, :, pl.ds(0, rows)],
            dst_ref=kv.at[c, :, pl.ds(rows * (1 + b), rows)],
            send_sem=kv_send.at[c, b], recv_sem=kv_recv.at[c, b],
            device_id={"ctx": peers[b]}, device_id_type=MESH,
        )

    def kv_edge(c):
        return pltpu.make_async_remote_copy(
            src_ref=kv.at[c, :, pl.ds(edge_first, BLOCK)],
            dst_ref=kv.at[c, :, pl.ds(edge_at, BLOCK)],
            send_sem=kv_send.at[c, bits], recv_sem=kv_recv.at[c, bits],
            device_id={"ctx": edge_peer}, device_id_type=MESH,
        )

    def term_copy(c, b):
        return pltpu.make_async_remote_copy(
            src_ref=terms.at[c, :, pl.ds(rows * b, rows)],
            dst_ref=back.at[c, :, pl.ds(rows * b, rows)],
            send_sem=t_send.at[c, b], recv_sem=t_recv.at[c, b],
            device_id={"ctx": peers[b]}, device_id_type=MESH,
        )

    def term_edge(c):
        return pltpu.make_async_remote_copy(
            src_ref=terms.at[c, :, pl.ds(rows * bits, BLOCK)],
            dst_ref=back.at[c, :, pl.ds(rows * bits, BLOCK)],
            send_sem=t_send.at[c, bits], recv_sem=t_recv.at[c, bits],
            device_id={"ctx": edge_peer}, device_id_type=MESH,
        )

    order = list(range(bits))[::-1]
    for c in range(chunks):
        for b in order:
            kv_copy(c, b).start()

        @pl.when(has_edge)
        def _():
            kv_edge(c).start()

    for copy in in_copies:
        copy.wait()
    for c in range(chunks):
        if total > glob_at + globals_:
            kv[c, :, glob_at + globals_ :] = jnp.zeros(
                (2, total - glob_at - globals_, LANES), kv.dtype
            )

    @pl.when(jnp.logical_not(has_edge))
    def _():
        kv[:, :, edge_at : edge_at + BLOCK] = jnp.zeros((chunks, 2, BLOCK, LANES), kv.dtype)
        back[:, :, rows * bits : rows * bits + BLOCK] = jnp.zeros(
            (chunks, 2, BLOCK, LANES), back.dtype
        )

    pair = 2 * rows
    query_block = lax.rem(lax.div(lax.broadcasted_iota(jnp.int32, (8, pair), 1), BLOCK), blocks)
    first_block = me * blocks
    listed = [
        [(ps_ref[r, first_block + n], pb_ref[r, first_block + n]) for r in range(R)]
        for n in range(blocks)
    ]

    def put_bias(at, counts):
        times = jnp.zeros((8, pair), jnp.int32)
        for n in range(blocks):
            times = jnp.where(query_block == n, counts[n], times)
        times = times.astype(jnp.float32)
        line = jnp.where(times > 0.5, jnp.log(jnp.maximum(times, 1.0)), MASKED)
        for step in range(BLOCK // 8):
            bias[at + step * 8 : at + step * 8 + 8] = line

    for j in range(blocks):
        put_bias(j * BLOCK, [jnp.int32(1 if abs(j - n) <= 1 else 0) for n in range(blocks)])
    for b in range(bits):
        for j in range(blocks):
            counts = []
            for n in range(blocks):
                times = jnp.int32(0)
                for shard, block in listed[n]:
                    times += jnp.where(shard == peers[b], 1, 0) * jnp.where(block == j, 1, 0)
                if b == 0 and j == 0 and n == blocks - 1:
                    times += 1 - odd
                if b == 0 and j == blocks - 1 and n == 0:
                    times += odd
                counts.append(times)
            put_bias(rows * (1 + b) + j * BLOCK, counts)
    valid = jnp.where(has_edge, 1, 0)
    edge_counts = [jnp.int32(0)] * blocks
    edge_counts[0] = edge_counts[0] + (1 - odd) * valid
    edge_counts[blocks - 1] = edge_counts[blocks - 1] + odd * valid
    put_bias(edge_at, edge_counts)
    for at in range(glob_at, glob_at + globals_, BLOCK):
        put_bias(at, [jnp.int32(1)] * blocks)
    if total > glob_at + globals_:
        bias[glob_at + globals_ :] = jnp.full((total - glob_at - globals_, pair), MASKED)

    low_head = lax.broadcasted_iota(jnp.int32, (rows, LANES), 1) < HEAD_DIM
    scaling = 1.0 / math.sqrt(HEAD_DIM)

    def both_heads(x):
        x = x.astype(jnp.float32)
        zero = jnp.zeros_like(x)
        return jnp.concatenate(
            [jnp.where(low_head, x, zero), jnp.where(low_head, zero, x)], axis=0
        )

    def dot(a, b, dims):
        return lax.dot_general(a, b, dims, preferred_element_type=jnp.float32)

    NN = (((1,), (0,)), ((), ()))

    def by_query(x):
        return jnp.concatenate([x[:HEAD_DIM, :rows], x[HEAD_DIM:, rows:]], axis=0).T

    def digit_of(i):
        axis, stride, radix, _ = stages[i]
        return lax.rem(lax.div(spot[axis], stride), radix)

    def peer_of(i, k):
        axis, stride, radix, _ = stages[i]
        digit = digit_of(i)
        other = lax.rem(digit + k, radix)
        return other, {axis: spot[axis] + (other - digit) * stride}

    def scatter_copy(i, k):
        held = stages[i][3]
        other, device = peer_of(i, k)
        at = other * held if accs[i].shape[0] != held else 0
        return pltpu.make_async_remote_copy(
            src_ref=accs[i].at[pl.ds(pl.multiple_of(at, 16), held)],
            dst_ref=recvs[i].at[k - 1],
            send_sem=rs_send[i].at[k - 1], recv_sem=rs_recv[i].at[k - 1],
            device_id=device, device_id_type=MESH,
        )

    def step(c, carry):
        lanes = pl.ds(pl.multiple_of(c * LANES, LANES), LANES)
        queries = (both_heads(q_ref[:, lanes]) * scaling).astype(jnp.bfloat16)
        grads = both_heads(u_ref[:, lanes]).astype(jnp.bfloat16)
        for b in order:
            kv_copy(c, b).wait_recv()

        @pl.when(has_edge)
        def _():
            kv_edge(c).wait_recv()

        keys = kv[c, 0]
        values = kv[c, 1]
        scores = dot(keys, queries, NT) + bias[...]
        weights = jnp.exp(scores - jnp.max(scores, axis=0, keepdims=True))
        probs = weights * (1.0 / jnp.sum(weights, axis=0, keepdims=True))
        low = probs.astype(jnp.bfloat16)
        dprobs = dot(values, grads, NT)
        inner = jnp.sum(probs * dprobs, axis=0, keepdims=True)
        dscores = (probs * (dprobs - inner)).astype(jnp.bfloat16)
        for which, (left, right) in enumerate(((dscores, queries), (low, grads))):
            made = dot(left, right, NN)
            own[c, which] = made[0:rows]
            terms[c, which] = made[rows:glob_at].astype(jnp.bfloat16)
            accs[0][
                pl.ds(pl.multiple_of((c * 2 + which) * globals_, globals_), globals_)
            ] = made[glob_at : glob_at + globals_].astype(jnp.bfloat16)
        for k in range(1, stages[0][2]):
            held = stages[0][3]
            ready = lax.div((peer_of(0, k)[0] + 1) * held - 1, 2 * globals_)
            if accs[0].shape[0] == held:
                ready = chunks - 1

            @pl.when(c == ready)
            def _(k=k):
                scatter_copy(0, k).start()

        for b in order:
            term_copy(c, b).start()

        @pl.when(has_edge)
        def _():
            term_edge(c).start()

        att_ref[:, lanes] = by_query(dot(values, low, TN)).astype(jnp.bfloat16)
        dq_ref[:, lanes] = (by_query(dot(keys, dscores, TN)) * scaling).astype(jnp.bfloat16)
        return carry

    lax.fori_loop(0, chunks, step, 0)
    out_copies = [
        pltpu.make_async_copy(ref, out, out_sem.at[i])
        for i, (ref, out) in enumerate(
            zip((att_ref, dq_ref, dk_ref, dv_ref, dgk_ref, dgv_ref), outs_hbm)
        )
    ]
    out_copies[0].start()
    out_copies[1].start()

    starts = []
    start = 0
    for i, (axis, stride, radix, held) in enumerate(stages):
        if accs[i].shape[0] != held:
            start = start + digit_of(i) * held
        starts.append(start)

    def scatter_start(i):
        for k in range(1, stages[i][2]):
            scatter_copy(i, k).start()

    def scatter_end(i):
        held = stages[i][3]
        at = digit_of(i) * held if accs[i].shape[0] != held else 0
        summed = accs[i][pl.ds(pl.multiple_of(at, 16), held)].astype(jnp.float32)
        for k in range(1, stages[i][2]):
            scatter_copy(i, k).wait_recv()
            summed = summed + recvs[i][k - 1].astype(jnp.float32)
        summed = summed.astype(jnp.bfloat16)
        if i + 1 < count:
            accs[i + 1][...] = summed
        else:
            final[pl.ds(pl.multiple_of(starts[i], 16), held)] = summed

    def gather_copy(i, k, at):
        held = stages[i][3]
        part = final.at[pl.ds(pl.multiple_of(at, 16), held)]
        return pltpu.make_async_remote_copy(
            src_ref=part, dst_ref=part,
            send_sem=ag_send[i].at[k - 1], recv_sem=ag_recv[i].at[k - 1],
            device_id=peer_of(i, k)[1], device_id_type=MESH,
        )

    def gather_start(i):
        for k in range(1, stages[i][2]):
            gather_copy(i, k, starts[i]).start()

    def gather_end(i):
        _, _, radix, held = stages[i]
        for k in range(1, radix):
            behind = lax.rem(digit_of(i) + radix - k, radix)
            gather_copy(i, k, starts[i] + (behind - digit_of(i)) * held).wait_recv()

    def collect(c):
        lanes = slice(c * LANES, (c + 1) * LANES)
        for b in order:
            term_copy(c, b).wait_recv()

        @pl.when(has_edge)
        def _():
            term_edge(c).wait_recv()

        low_rows = lax.broadcasted_iota(jnp.int32, (rows, LANES), 0)
        at_edge = jnp.logical_and(low_rows >= edge_first, low_rows < edge_first + BLOCK)
        for which, out in enumerate((dk_ref, dv_ref)):
            summed = own[c, which]
            for b in range(bits):
                summed = summed + back[c, which, rows * b : rows * (b + 1)].astype(jnp.float32)
            edge = back[c, which, rows * bits : rows * bits + BLOCK].astype(jnp.float32)
            edge = jnp.concatenate([edge] * blocks, axis=0)
            summed = summed + jnp.where(at_edge, edge, 0.0)
            out[:, lanes] = summed.astype(jnp.bfloat16)

    for i in range(count):
        if i:
            scatter_start(i)
        scatter_end(i)
    split = [i for i in range(count) if accs[i].shape[0] != stages[i][3]]
    todo = list(range(chunks))
    for i in split[::-1]:
        gather_start(i)
        if todo:
            collect(todo.pop(0))
        gather_end(i)
    for c in range(chunks):
        lanes = slice(c * LANES, (c + 1) * LANES)
        for which, out in enumerate((dgk_ref, dgv_ref)):
            at = (c * 2 + which) * globals_
            out[:, lanes] = final[at : at + globals_].astype(jnp.float32)
    out_copies[4].start()
    out_copies[5].start()
    for c in todo:
        collect(c)
    out_copies[2].start()
    out_copies[3].start()

    for c in range(chunks):
        for b in order:
            kv_copy(c, b).wait_send()
            term_copy(c, b).wait_send()

        @pl.when(has_edge)
        def _():
            kv_edge(c).wait_send()
            term_edge(c).wait_send()

    for i in range(count):
        for k in range(1, stages[i][2]):
            scatter_copy(i, k).wait_send()
            if i in split:
                gather_copy(i, k, starts[i]).wait_send()

    for copy in out_copies:
        copy.wait()


def write_out(*refs):
    count = len(refs) // 2
    copies = [
        pltpu.make_async_copy(refs[i], refs[count + i], refs[-1].at[i]) for i in range(count)
    ]
    for copy in copies:
        copy.start()
    for copy in copies:
        copy.wait()


def body(shards, replicas, queries, keys, values, global_keys, global_values, upstream, ps, pb):
    _, rows, width = queries.shape
    globals_ = global_keys.shape[0]
    bits = shards.bit_length() - 1
    chunks = width // LANES
    used = rows * (1 + bits) + BLOCK + globals_
    total = -(-used // LANES) * LANES
    gathered = 2 * chunks * globals_
    stages = reduce_stages((("dp", replicas), ("ctx", shards)), gathered)
    low = jnp.bfloat16
    accs, recvs, sems = [], [], []
    held = gathered
    for _, _, radix, after in stages:
        accs.append(pltpu.VMEM((held, LANES), low))
        recvs.append(pltpu.VMEM((radix - 1, after, LANES), low))
        sems.append(pltpu.SemaphoreType.DMA((radix - 1,)))
        held = after
    hbm = pl.BlockSpec(memory_space=pltpu.HBM)
    dma = pltpu.SemaphoreType.DMA((chunks, bits + 1))
    remote = rows * bits + BLOCK
    results = [((rows, width), low)] * 4 + [((globals_, width), jnp.float32)] * 2
    outs = pl.pallas_call(
        functools.partial(kernel, shards, stages),
        out_shape=[jax.ShapeDtypeStruct(*x) for x in results],
        in_specs=[hbm] * 8,
        out_specs=[hbm] * 6,
        scratch_shapes=[
            *[pltpu.VMEM(*x) for x in results],
            pltpu.SemaphoreType.DMA((6,)),
            pltpu.VMEM((rows, width), low),
            pltpu.VMEM((rows, width), low),
            pltpu.SMEM(ps.T.shape, jnp.int32),
            pltpu.SMEM(pb.T.shape, jnp.int32),
            pltpu.SemaphoreType.DMA((4,)),
            pltpu.SemaphoreType.DMA((2, chunks, 2)),
            pltpu.VMEM((chunks, 2, total, LANES), low),
            pltpu.VMEM((total, 2 * rows), jnp.float32),
            pltpu.VMEM((chunks, 2, remote, LANES), low),
            pltpu.VMEM((chunks, 2, remote, LANES), low),
            pltpu.VMEM((chunks, 2, rows, LANES), jnp.float32),
            *accs,
            *recvs,
            pltpu.VMEM((gathered, LANES), low),
            dma, dma, dma, dma,
            *sems, *sems, *sems, *sems,
        ],
        compiler_params=pltpu.CompilerParams(
            collective_id=0, has_side_effects=True, vmem_limit_bytes=VMEM_BYTES
        ),
    )(queries[0], keys[0], values[0], global_keys, global_values, upstream[0], ps.T, pb.T)
    outs = pl.pallas_call(
        write_out,
        out_shape=[jax.ShapeDtypeStruct(x.shape, x.dtype) for x in outs],
        in_specs=[hbm] * 6,
        out_specs=[hbm] * 6,
        scratch_shapes=[pltpu.SemaphoreType.DMA((6,))],
        compiler_params=pltpu.CompilerParams(vmem_limit_bytes=VMEM_BYTES),
    )(*outs)
    return (outs[0][None], outs[1][None], outs[2][None], outs[3][None], outs[4], outs[5])


def solution(mesh):
    split = P("dp", "ctx", None)
    return jax.shard_map(
        functools.partial(body, mesh.shape["ctx"], mesh.shape["dp"]),
        mesh=mesh,
        in_specs=(split, split, split, P(), P(), split, P(), P()),
        out_specs=(split, split, split, split, P(), P()),
        check_vma=False,
    )
```

```python
import functools
import math

import jax
import jax.numpy as jnp
from jax import lax
from jax.experimental import pallas as pl
from jax.experimental.pallas import tpu as pltpu
from jax.sharding import PartitionSpec as P

HEAD_DIM = 64
BLOCK = 64
R = 3
LANES = 128
VMEM_BYTES = 63 * 1024 * 1024
MASKED = -1e30
MESH = pl.DeviceIdType.MESH
NT = (((1,), (1,)), ((), ()))
TN = (((0,), (0,)), ((), ()))


def reduce_stages(sizes, rows):
    stages = []
    for axis, size in sizes:
        stride = 1
        while stride < size:
            radix = min(8, size // stride)
            if rows % (radix * 16) == 0:
                rows //= radix
            stages.append((axis, stride, radix, rows))
            stride *= radix
    return stages


def kernel(
    shards, stages, q_hbm, k_hbm, v_hbm, gk_hbm, gv_hbm, u_hbm, ps_hbm, pb_hbm,
    *refs,
):
    outs_hbm, (att_ref, dq_ref, dk_ref, dv_ref, dgk_ref, dgv_ref) = refs[:6], refs[6:12]
    run(
        shards, stages, q_hbm, k_hbm, v_hbm, gk_hbm, gv_hbm, u_hbm, ps_hbm, pb_hbm, outs_hbm,
        att_ref, dq_ref, dk_ref, dv_ref, dgk_ref, dgv_ref, *refs[12:],
    )


def run(
    shards, stages, q_hbm, k_hbm, v_hbm, gk_hbm, gv_hbm, u_hbm, ps_hbm, pb_hbm, outs_hbm,
    att_ref, dq_ref, dk_ref, dv_ref, dgk_ref, dgv_ref, out_sem,
    q_ref, u_ref, ps_ref, pb_ref, in_sem, own_sem, kv, bias, terms, back, own, *rest,
):
    count = len(stages)
    accs, recvs = rest[:count], rest[count : 2 * count]
    final = rest[2 * count]
    kv_send, kv_recv, t_send, t_recv = rest[2 * count + 1 : 2 * count + 5]
    sems = rest[2 * count + 5 :]
    rs_send, rs_recv = sems[:count], sems[count : 2 * count]
    ag_send, ag_recv = sems[2 * count : 3 * count], sems[3 * count :]

    rows, width = q_hbm.shape
    blocks = rows // BLOCK
    chunks = width // LANES
    bits = shards.bit_length() - 1
    globals_ = gk_hbm.shape[0]
    edge_at = rows * (1 + bits)
    glob_at = edge_at + BLOCK
    total = kv.shape[2]
    me = lax.axis_index("ctx")
    spot = {"ctx": me, "dp": lax.axis_index("dp")}
    odd = lax.rem(me, 2)
    edge_peer = me - 1 + 2 * odd
    has_edge = jnp.logical_and(edge_peer >= 0, edge_peer < shards)
    edge_first = pl.multiple_of(odd * (rows - BLOCK), BLOCK)
    peers = [me + (1 << b) * (1 - 2 * lax.rem(lax.div(me, 1 << b), 2)) for b in range(bits)]

    barrier = pltpu.get_barrier_semaphore()

    def greet(axis, to):
        pl.semaphore_signal(barrier, inc=1, device_id={axis: to}, device_id_type=MESH)

    greeted = 0
    for axis, stride, radix, _ in stages:
        digit = lax.rem(lax.div(spot[axis], stride), radix)
        for k in range(1, radix):
            greet(axis, spot[axis] + (lax.rem(digit + k, radix) - digit) * stride)
            greeted += 1

    apart = all(radix < shards for axis, _, radix, _ in stages if axis == "ctx")
    if apart:

        @pl.when(has_edge)
        def _():
            greet("ctx", edge_peer)

    own_copies, in_copies = [], []
    for c in range(chunks):
        lanes = pl.ds(c * LANES, LANES)
        for which, (part, shared) in enumerate(((k_hbm, gk_hbm), (v_hbm, gv_hbm))):
            own_copies.append(
                pltpu.make_async_copy(
                    part.at[:, lanes], kv.at[c, which, pl.ds(0, rows)], own_sem.at[0, c, which]
                )
            )
            in_copies.append(
                pltpu.make_async_copy(
                    shared.at[:, lanes],
                    kv.at[c, which, pl.ds(glob_at, globals_)],
                    own_sem.at[1, c, which],
                )
            )
    for i, (src, dst) in enumerate(
        ((ps_hbm, ps_ref), (pb_hbm, pb_ref), (q_hbm, q_ref), (u_hbm, u_ref))
    ):
        in_copies.append(pltpu.make_async_copy(src, dst, in_sem.at[i]))
    for copy in own_copies + in_copies:
        copy.start()
    for copy in own_copies:
        copy.wait()

    pl.semaphore_wait(barrier, greeted + jnp.where(has_edge, 1, 0) if apart else greeted)

    def kv_copy(c, b):
        return pltpu.make_async_remote_copy(
            src_ref=kv.at[c, :, pl.ds(0, rows)],
            dst_ref=kv.at[c, :, pl.ds(rows * (1 + b), rows)],
            send_sem=kv_send.at[c, b], recv_sem=kv_recv.at[c, b],
            device_id={"ctx": peers[b]}, device_id_type=MESH,
        )

    def kv_edge(c):
        return pltpu.make_async_remote_copy(
            src_ref=kv.at[c, :, pl.ds(edge_first, BLOCK)],
            dst_ref=kv.at[c, :, pl.ds(edge_at, BLOCK)],
            send_sem=kv_send.at[c, bits], recv_sem=kv_recv.at[c, bits],
            device_id={"ctx": edge_peer}, device_id_type=MESH,
        )

    def term_copy(c, b):
        return pltpu.make_async_remote_copy(
            src_ref=terms.at[c, :, pl.ds(rows * b, rows)],
            dst_ref=back.at[c, :, pl.ds(rows * b, rows)],
            send_sem=t_send.at[c, b], recv_sem=t_recv.at[c, b],
            device_id={"ctx": peers[b]}, device_id_type=MESH,
        )

    def term_edge(c):
        return pltpu.make_async_remote_copy(
            src_ref=terms.at[c, :, pl.ds(rows * bits, BLOCK)],
            dst_ref=back.at[c, :, pl.ds(rows * bits, BLOCK)],
            send_sem=t_send.at[c, bits], recv_sem=t_recv.at[c, bits],
            device_id={"ctx": edge_peer}, device_id_type=MESH,
        )

    order = list(range(bits))[::-1]

    def send_kv(c):
        for b in order:
            kv_copy(c, b).start()

        @pl.when(has_edge)
        def _():
            kv_edge(c).start()

    def send_terms(c):
        for b in order:
            term_copy(c, b).start()

        @pl.when(has_edge)
        def _():
            term_edge(c).start()

    ahead = min(2, chunks)
    for c in range(ahead):
        send_kv(c)

    for copy in in_copies:
        copy.wait()
    for c in range(chunks):
        if total > glob_at + globals_:
            kv[c, :, glob_at + globals_ :] = jnp.zeros(
                (2, total - glob_at - globals_, LANES), kv.dtype
            )

    @pl.when(jnp.logical_not(has_edge))
    def _():
        kv[:, :, edge_at : edge_at + BLOCK] = jnp.zeros((chunks, 2, BLOCK, LANES), kv.dtype)
        back[:, :, rows * bits : rows * bits + BLOCK] = jnp.zeros(
            (chunks, 2, BLOCK, LANES), back.dtype
        )

    pair = 2 * rows
    query_block = lax.rem(lax.div(lax.broadcasted_iota(jnp.int32, (8, pair), 1), BLOCK), blocks)
    first_block = me * blocks
    listed = [
        [(ps_ref[r, first_block + n], pb_ref[r, first_block + n]) for r in range(R)]
        for n in range(blocks)
    ]

    def put_bias(at, counts):
        times = jnp.zeros((8, pair), jnp.int32)
        for n in range(blocks):
            times = jnp.where(query_block == n, counts[n], times)
        times = times.astype(jnp.float32)
        line = jnp.where(times > 0.5, jnp.log(jnp.maximum(times, 1.0)), MASKED)
        for step in range(BLOCK // 8):
            bias[at + step * 8 : at + step * 8 + 8] = line

    for j in range(blocks):
        put_bias(j * BLOCK, [jnp.int32(1 if abs(j - n) <= 1 else 0) for n in range(blocks)])
    for b in range(bits):
        for j in range(blocks):
            counts = []
            for n in range(blocks):
                times = jnp.int32(0)
                for shard, block in listed[n]:
                    times += jnp.where(shard == peers[b], 1, 0) * jnp.where(block == j, 1, 0)
                if b == 0 and j == 0 and n == blocks - 1:
                    times += 1 - odd
                if b == 0 and j == blocks - 1 and n == 0:
                    times += odd
                counts.append(times)
            put_bias(rows * (1 + b) + j * BLOCK, counts)
    valid = jnp.where(has_edge, 1, 0)
    edge_counts = [jnp.int32(0)] * blocks
    edge_counts[0] = edge_counts[0] + (1 - odd) * valid
    edge_counts[blocks - 1] = edge_counts[blocks - 1] + odd * valid
    put_bias(edge_at, edge_counts)
    for at in range(glob_at, glob_at + globals_, BLOCK):
        put_bias(at, [jnp.int32(1)] * blocks)
    if total > glob_at + globals_:
        bias[glob_at + globals_ :] = jnp.full((total - glob_at - globals_, pair), MASKED)

    low_head = lax.broadcasted_iota(jnp.int32, (rows, LANES), 1) < HEAD_DIM
    scaling = 1.0 / math.sqrt(HEAD_DIM)

    def both_heads(x):
        x = x.astype(jnp.float32)
        zero = jnp.zeros_like(x)
        return jnp.concatenate(
            [jnp.where(low_head, x, zero), jnp.where(low_head, zero, x)], axis=0
        )

    def dot(a, b, dims):
        return lax.dot_general(a, b, dims, preferred_element_type=jnp.float32)

    NN = (((1,), (0,)), ((), ()))

    def by_query(x):
        return jnp.concatenate([x[:HEAD_DIM, :rows], x[HEAD_DIM:, rows:]], axis=0).T

    def digit_of(i):
        axis, stride, radix, _ = stages[i]
        return lax.rem(lax.div(spot[axis], stride), radix)

    def peer_of(i, k):
        axis, stride, radix, _ = stages[i]
        digit = digit_of(i)
        other = lax.rem(digit + k, radix)
        return other, {axis: spot[axis] + (other - digit) * stride}

    def scatter_copy(i, k):
        held = stages[i][3]
        other, device = peer_of(i, k)
        at = other * held if accs[i].shape[0] != held else 0
        return pltpu.make_async_remote_copy(
            src_ref=accs[i].at[pl.ds(pl.multiple_of(at, 16), held)],
            dst_ref=recvs[i].at[k - 1],
            send_sem=rs_send[i].at[k - 1], recv_sem=rs_recv[i].at[k - 1],
            device_id=device, device_id_type=MESH,
        )

    def step(c, carry):
        lanes = pl.ds(pl.multiple_of(c * LANES, LANES), LANES)
        queries = (both_heads(q_ref[:, lanes]) * scaling).astype(jnp.bfloat16)
        grads = both_heads(u_ref[:, lanes]).astype(jnp.bfloat16)
        for b in order:
            kv_copy(c, b).wait_recv()

        @pl.when(has_edge)
        def _():
            kv_edge(c).wait_recv()

        @pl.when(c + ahead < chunks)
        def _():
            send_kv(c + ahead)

        keys = kv[c, 0]
        values = kv[c, 1]
        scores = dot(keys, queries, NT) + bias[...]
        weights = jnp.exp(scores - jnp.max(scores, axis=0, keepdims=True))
        probs = weights * (1.0 / jnp.sum(weights, axis=0, keepdims=True))
        low = probs.astype(jnp.bfloat16)
        dprobs = dot(values, grads, NT)
        inner = jnp.sum(probs * dprobs, axis=0, keepdims=True)
        dscores = (probs * (dprobs - inner)).astype(jnp.bfloat16)
        for which, (left, right) in enumerate(((dscores, queries), (low, grads))):
            made = dot(left, right, NN)
            own[c, which] = made[0:rows]
            terms[c, which] = made[rows:glob_at].astype(jnp.bfloat16)
            accs[0][
                pl.ds(pl.multiple_of((c * 2 + which) * globals_, globals_), globals_)
            ] = made[glob_at : glob_at + globals_].astype(jnp.bfloat16)
        for k in range(1, stages[0][2]):
            held = stages[0][3]
            ready = lax.div((peer_of(0, k)[0] + 1) * held - 1, 2 * globals_)
            if accs[0].shape[0] == held:
                ready = chunks - 1

            @pl.when(c == ready)
            def _(k=k):
                scatter_copy(0, k).start()

        @pl.when(c < chunks - 2)
        def _():
            send_terms(c)

        att_ref[:, lanes] = by_query(dot(values, low, TN)).astype(jnp.bfloat16)
        dq_ref[:, lanes] = (by_query(dot(keys, dscores, TN)) * scaling).astype(jnp.bfloat16)
        return carry

    lax.fori_loop(0, chunks, step, 0)
    out_copies = [
        pltpu.make_async_copy(ref, out, out_sem.at[i])
        for i, (ref, out) in enumerate(
            zip((att_ref, dq_ref, dk_ref, dv_ref, dgk_ref, dgv_ref), outs_hbm)
        )
    ]
    out_copies[0].start()
    out_copies[1].start()

    starts = []
    start = 0
    for i, (axis, stride, radix, held) in enumerate(stages):
        if accs[i].shape[0] != held:
            start = start + digit_of(i) * held
        starts.append(start)

    def scatter_start(i):
        for k in range(1, stages[i][2]):
            scatter_copy(i, k).start()

    def scatter_end(i):
        held = stages[i][3]
        at = digit_of(i) * held if accs[i].shape[0] != held else 0
        summed = accs[i][pl.ds(pl.multiple_of(at, 16), held)].astype(jnp.float32)
        for k in range(1, stages[i][2]):
            scatter_copy(i, k).wait_recv()
            summed = summed + recvs[i][k - 1].astype(jnp.float32)
        summed = summed.astype(jnp.bfloat16)
        if i + 1 < count:
            accs[i + 1][...] = summed
        else:
            final[pl.ds(pl.multiple_of(starts[i], 16), held)] = summed

    def gather_copy(i, k, at):
        held = stages[i][3]
        part = final.at[pl.ds(pl.multiple_of(at, 16), held)]
        return pltpu.make_async_remote_copy(
            src_ref=part, dst_ref=part,
            send_sem=ag_send[i].at[k - 1], recv_sem=ag_recv[i].at[k - 1],
            device_id=peer_of(i, k)[1], device_id_type=MESH,
        )

    def gather_start(i):
        for k in range(1, stages[i][2]):
            gather_copy(i, k, starts[i]).start()

    def gather_end(i):
        _, _, radix, held = stages[i]
        for k in range(1, radix):
            behind = lax.rem(digit_of(i) + radix - k, radix)
            gather_copy(i, k, starts[i] + (behind - digit_of(i)) * held).wait_recv()

    def collect(c):
        lanes = slice(c * LANES, (c + 1) * LANES)
        for b in order:
            term_copy(c, b).wait_recv()

        @pl.when(has_edge)
        def _():
            term_edge(c).wait_recv()

        low_rows = lax.broadcasted_iota(jnp.int32, (rows, LANES), 0)
        at_edge = jnp.logical_and(low_rows >= edge_first, low_rows < edge_first + BLOCK)
        for which, out in enumerate((dk_ref, dv_ref)):
            summed = own[c, which]
            for b in range(bits):
                summed = summed + back[c, which, rows * b : rows * (b + 1)].astype(jnp.float32)
            edge = back[c, which, rows * bits : rows * bits + BLOCK].astype(jnp.float32)
            edge = jnp.concatenate([edge] * blocks, axis=0)
            summed = summed + jnp.where(at_edge, edge, 0.0)
            out[:, lanes] = summed.astype(jnp.bfloat16)

    for i in range(count):
        if i:
            scatter_start(i)
        if i == count - 1 and chunks > 1:
            send_terms(chunks - 2)
        scatter_end(i)
    split = [i for i in range(count) if accs[i].shape[0] != stages[i][3]]
    todo = list(range(chunks))
    for i in split[::-1]:
        gather_start(i)
        if i == split[-1]:
            send_terms(chunks - 1)
        if todo:
            collect(todo.pop(0))
        gather_end(i)
    for c in range(chunks):
        lanes = slice(c * LANES, (c + 1) * LANES)
        for which, out in enumerate((dgk_ref, dgv_ref)):
            at = (c * 2 + which) * globals_
            out[:, lanes] = final[at : at + globals_].astype(jnp.float32)
    out_copies[4].start()
    out_copies[5].start()
    for c in todo:
        collect(c)
    out_copies[2].start()
    out_copies[3].start()

    for c in range(chunks):
        for b in order:
            kv_copy(c, b).wait_send()
            term_copy(c, b).wait_send()

        @pl.when(has_edge)
        def _():
            kv_edge(c).wait_send()
            term_edge(c).wait_send()

    for i in range(count):
        for k in range(1, stages[i][2]):
            scatter_copy(i, k).wait_send()
            if i in split:
                gather_copy(i, k, starts[i]).wait_send()

    for copy in out_copies:
        copy.wait()


def write_out(*refs):
    count = len(refs) // 3
    sem = refs[-1]
    loads = [
        pltpu.make_async_copy(refs[i], refs[2 * count + i], sem.at[0, i]) for i in range(count)
    ]
    stores = [
        pltpu.make_async_copy(refs[2 * count + i], refs[count + i], sem.at[1, i])
        for i in range(count)
    ]
    for copy in loads:
        copy.start()
    for load, store in zip(loads, stores):
        load.wait()
        store.start()
    for copy in stores:
        copy.wait()


def body(shards, replicas, queries, keys, values, global_keys, global_values, upstream, ps, pb):
    _, rows, width = queries.shape
    globals_ = global_keys.shape[0]
    bits = shards.bit_length() - 1
    chunks = width // LANES
    used = rows * (1 + bits) + BLOCK + globals_
    total = -(-used // LANES) * LANES
    gathered = 2 * chunks * globals_
    stages = reduce_stages((("dp", replicas), ("ctx", shards)), gathered)
    low = jnp.bfloat16
    accs, recvs, sems = [], [], []
    held = gathered
    for _, _, radix, after in stages:
        accs.append(pltpu.VMEM((held, LANES), low))
        recvs.append(pltpu.VMEM((radix - 1, after, LANES), low))
        sems.append(pltpu.SemaphoreType.DMA((radix - 1,)))
        held = after
    hbm = pl.BlockSpec(memory_space=pltpu.HBM)
    dma = pltpu.SemaphoreType.DMA((chunks, bits + 1))
    remote = rows * bits + BLOCK
    results = [((rows, width), low)] * 4 + [((globals_, width), jnp.float32)] * 2
    outs = pl.pallas_call(
        functools.partial(kernel, shards, stages),
        out_shape=[jax.ShapeDtypeStruct(*x) for x in results],
        in_specs=[hbm] * 8,
        out_specs=[hbm] * 6,
        scratch_shapes=[
            *[pltpu.VMEM(*x) for x in results],
            pltpu.SemaphoreType.DMA((6,)),
            pltpu.VMEM((rows, width), low),
            pltpu.VMEM((rows, width), low),
            pltpu.SMEM(ps.T.shape, jnp.int32),
            pltpu.SMEM(pb.T.shape, jnp.int32),
            pltpu.SemaphoreType.DMA((4,)),
            pltpu.SemaphoreType.DMA((2, chunks, 2)),
            pltpu.VMEM((chunks, 2, total, LANES), low),
            pltpu.VMEM((total, 2 * rows), jnp.float32),
            pltpu.VMEM((chunks, 2, remote, LANES), low),
            pltpu.VMEM((chunks, 2, remote, LANES), low),
            pltpu.VMEM((chunks, 2, rows, LANES), jnp.float32),
            *accs,
            *recvs,
            pltpu.VMEM((gathered, LANES), low),
            dma, dma, dma, dma,
            *sems, *sems, *sems, *sems,
        ],
        compiler_params=pltpu.CompilerParams(
            collective_id=0, has_side_effects=True, vmem_limit_bytes=VMEM_BYTES
        ),
    )(queries[0], keys[0], values[0], global_keys, global_values, upstream[0], ps.T, pb.T)
    outs = pl.pallas_call(
        write_out,
        out_shape=[jax.ShapeDtypeStruct(x.shape, x.dtype) for x in outs],
        in_specs=[hbm] * 6,
        out_specs=[hbm] * 6,
        scratch_shapes=[
            *[pltpu.VMEM(*x) for x in results],
            pltpu.SemaphoreType.DMA((2, 6)),
        ],
        compiler_params=pltpu.CompilerParams(vmem_limit_bytes=VMEM_BYTES),
    )(*outs)
    return (outs[0][None], outs[1][None], outs[2][None], outs[3][None], outs[4], outs[5])


def solution(mesh):
    split = P("dp", "ctx", None)
    return jax.shard_map(
        functools.partial(body, mesh.shape["ctx"], mesh.shape["dp"]),
        mesh=mesh,
        in_specs=(split, split, split, P(), P(), split, P(), P()),
        out_specs=(split, split, split, split, P(), P()),
        check_vma=False,
    )
```

```python
import functools
import math

import jax
import jax.numpy as jnp
from jax import lax
from jax.experimental import pallas as pl
from jax.experimental.pallas import tpu as pltpu
from jax.sharding import PartitionSpec as P

HEAD_DIM = 64
BLOCK = 64
R = 3
LANES = 128
VMEM_BYTES = 63 * 1024 * 1024
MASKED = -1e30
MESH = pl.DeviceIdType.MESH
NT = (((1,), (1,)), ((), ()))
TN = (((0,), (0,)), ((), ()))


def reduce_stages(sizes, rows):
    stages = []
    for axis, size in sizes:
        stride = 1
        while stride < size:
            radix = min(8, size // stride)
            if rows % (radix * 16) == 0:
                rows //= radix
            stages.append((axis, stride, radix, rows))
            stride *= radix
    return stages


def kernel(
    shards, stages, q_hbm, k_hbm, v_hbm, gk_hbm, gv_hbm, u_hbm, ps_hbm, pb_hbm,
    *refs,
):
    outs_hbm, (att_ref, dq_ref, dk_ref, dv_ref, dgk_ref, dgv_ref) = refs[:6], refs[6:12]
    run(
        shards, stages, q_hbm, k_hbm, v_hbm, gk_hbm, gv_hbm, u_hbm, ps_hbm, pb_hbm, outs_hbm,
        att_ref, dq_ref, dk_ref, dv_ref, dgk_ref, dgv_ref, *refs[12:],
    )


def run(
    shards, stages, q_hbm, k_hbm, v_hbm, gk_hbm, gv_hbm, u_hbm, ps_hbm, pb_hbm, outs_hbm,
    att_ref, dq_ref, dk_ref, dv_ref, dgk_ref, dgv_ref, out_sem,
    q_ref, u_ref, ps_ref, pb_ref, in_sem, own_sem, kv, bias, terms, back, own, *rest,
):
    count = len(stages)
    accs, recvs = rest[:count], rest[count : 2 * count]
    final = rest[2 * count]
    kv_send, kv_recv, t_send, t_recv = rest[2 * count + 1 : 2 * count + 5]
    sems = rest[2 * count + 5 :]
    rs_send, rs_recv = sems[:count], sems[count : 2 * count]
    ag_send, ag_recv = sems[2 * count : 3 * count], sems[3 * count :]

    rows, width = q_hbm.shape
    blocks = rows // BLOCK
    chunks = width // LANES
    bits = shards.bit_length() - 1
    globals_ = gk_hbm.shape[0]
    edge_at = rows * (1 + bits)
    glob_at = edge_at + BLOCK
    total = kv.shape[2]
    me = lax.axis_index("ctx")
    spot = {"ctx": me, "dp": lax.axis_index("dp")}
    odd = lax.rem(me, 2)
    edge_peer = me - 1 + 2 * odd
    has_edge = jnp.logical_and(edge_peer >= 0, edge_peer < shards)
    edge_first = pl.multiple_of(odd * (rows - BLOCK), BLOCK)
    peers = [me + (1 << b) * (1 - 2 * lax.rem(lax.div(me, 1 << b), 2)) for b in range(bits)]

    barrier = pltpu.get_barrier_semaphore()

    def greet(axis, to):
        pl.semaphore_signal(barrier, inc=1, device_id={axis: to}, device_id_type=MESH)

    greeted = 0
    for axis, stride, radix, _ in stages:
        digit = lax.rem(lax.div(spot[axis], stride), radix)
        for k in range(1, radix):
            greet(axis, spot[axis] + (lax.rem(digit + k, radix) - digit) * stride)
            greeted += 1

    apart = all(radix < shards for axis, _, radix, _ in stages if axis == "ctx")
    if apart:

        @pl.when(has_edge)
        def _():
            greet("ctx", edge_peer)

    own_copies, in_copies = [], []
    for c in range(chunks):
        lanes = pl.ds(c * LANES, LANES)
        for which, (part, shared) in enumerate(((k_hbm, gk_hbm), (v_hbm, gv_hbm))):
            own_copies.append(
                pltpu.make_async_copy(
                    part.at[:, lanes], kv.at[c, which, pl.ds(0, rows)], own_sem.at[0, c, which]
                )
            )
            in_copies.append(
                pltpu.make_async_copy(
                    shared.at[:, lanes],
                    kv.at[c, which, pl.ds(glob_at, globals_)],
                    own_sem.at[1, c, which],
                )
            )
    for i, (src, dst) in enumerate(
        ((ps_hbm, ps_ref), (pb_hbm, pb_ref), (q_hbm, q_ref), (u_hbm, u_ref))
    ):
        in_copies.append(pltpu.make_async_copy(src, dst, in_sem.at[i]))
    for copy in own_copies + in_copies:
        copy.start()
    for copy in own_copies:
        copy.wait()

    pl.semaphore_wait(barrier, greeted + jnp.where(has_edge, 1, 0) if apart else greeted)

    def kv_copy(c, b):
        return pltpu.make_async_remote_copy(
            src_ref=kv.at[c, :, pl.ds(0, rows)],
            dst_ref=kv.at[c, :, pl.ds(rows * (1 + b), rows)],
            send_sem=kv_send.at[c, b], recv_sem=kv_recv.at[c, b],
            device_id={"ctx": peers[b]}, device_id_type=MESH,
        )

    def kv_edge(c):
        return pltpu.make_async_remote_copy(
            src_ref=kv.at[c, :, pl.ds(edge_first, BLOCK)],
            dst_ref=kv.at[c, :, pl.ds(edge_at, BLOCK)],
            send_sem=kv_send.at[c, bits], recv_sem=kv_recv.at[c, bits],
            device_id={"ctx": edge_peer}, device_id_type=MESH,
        )

    def term_copy(c, b):
        return pltpu.make_async_remote_copy(
            src_ref=terms.at[c, :, pl.ds(rows * b, rows)],
            dst_ref=back.at[c, :, pl.ds(rows * b, rows)],
            send_sem=t_send.at[c, b], recv_sem=t_recv.at[c, b],
            device_id={"ctx": peers[b]}, device_id_type=MESH,
        )

    def term_edge(c):
        return pltpu.make_async_remote_copy(
            src_ref=terms.at[c, :, pl.ds(rows * bits, BLOCK)],
            dst_ref=back.at[c, :, pl.ds(rows * bits, BLOCK)],
            send_sem=t_send.at[c, bits], recv_sem=t_recv.at[c, bits],
            device_id={"ctx": edge_peer}, device_id_type=MESH,
        )

    order = list(range(bits))[::-1]

    def send_kv(c):
        for b in order:
            kv_copy(c, b).start()

        @pl.when(has_edge)
        def _():
            kv_edge(c).start()

    def send_terms(c):
        for b in order:
            term_copy(c, b).start()

        @pl.when(has_edge)
        def _():
            term_edge(c).start()

    ahead = min(2, chunks)
    send_kv(0)

    for copy in in_copies:
        copy.wait()
    for c in range(chunks):
        if total > glob_at + globals_:
            kv[c, :, glob_at + globals_ :] = jnp.zeros(
                (2, total - glob_at - globals_, LANES), kv.dtype
            )

    @pl.when(jnp.logical_not(has_edge))
    def _():
        kv[:, :, edge_at : edge_at + BLOCK] = jnp.zeros((chunks, 2, BLOCK, LANES), kv.dtype)
        back[:, :, rows * bits : rows * bits + BLOCK] = jnp.zeros(
            (chunks, 2, BLOCK, LANES), back.dtype
        )

    pair = 2 * rows
    query_block = lax.rem(lax.div(lax.broadcasted_iota(jnp.int32, (8, pair), 1), BLOCK), blocks)
    first_block = me * blocks
    listed = [
        [(ps_ref[r, first_block + n], pb_ref[r, first_block + n]) for r in range(R)]
        for n in range(blocks)
    ]

    def put_bias(at, counts):
        times = jnp.zeros((8, pair), jnp.int32)
        for n in range(blocks):
            times = jnp.where(query_block == n, counts[n], times)
        times = times.astype(jnp.float32)
        line = jnp.where(times > 0.5, jnp.log(jnp.maximum(times, 1.0)), MASKED)
        for step in range(BLOCK // 8):
            bias[at + step * 8 : at + step * 8 + 8] = line

    for j in range(blocks):
        put_bias(j * BLOCK, [jnp.int32(1 if abs(j - n) <= 1 else 0) for n in range(blocks)])
    for b in range(bits):
        for j in range(blocks):
            counts = []
            for n in range(blocks):
                times = jnp.int32(0)
                for shard, block in listed[n]:
                    times += jnp.where(shard == peers[b], 1, 0) * jnp.where(block == j, 1, 0)
                if b == 0 and j == 0 and n == blocks - 1:
                    times += 1 - odd
                if b == 0 and j == blocks - 1 and n == 0:
                    times += odd
                counts.append(times)
            put_bias(rows * (1 + b) + j * BLOCK, counts)
    valid = jnp.where(has_edge, 1, 0)
    edge_counts = [jnp.int32(0)] * blocks
    edge_counts[0] = edge_counts[0] + (1 - odd) * valid
    edge_counts[blocks - 1] = edge_counts[blocks - 1] + odd * valid
    put_bias(edge_at, edge_counts)
    for at in range(glob_at, glob_at + globals_, BLOCK):
        put_bias(at, [jnp.int32(1)] * blocks)
    if total > glob_at + globals_:
        bias[glob_at + globals_ :] = jnp.full((total - glob_at - globals_, pair), MASKED)

    low_head = lax.broadcasted_iota(jnp.int32, (rows, LANES), 1) < HEAD_DIM
    scaling = 1.0 / math.sqrt(HEAD_DIM)

    def both_heads(x):
        x = x.astype(jnp.float32)
        zero = jnp.zeros_like(x)
        return jnp.concatenate(
            [jnp.where(low_head, x, zero), jnp.where(low_head, zero, x)], axis=0
        )

    def dot(a, b, dims):
        return lax.dot_general(a, b, dims, preferred_element_type=jnp.float32)

    NN = (((1,), (0,)), ((), ()))

    def by_query(x):
        return jnp.concatenate([x[:HEAD_DIM, :rows], x[HEAD_DIM:, rows:]], axis=0).T

    def digit_of(i):
        axis, stride, radix, _ = stages[i]
        return lax.rem(lax.div(spot[axis], stride), radix)

    def peer_of(i, k):
        axis, stride, radix, _ = stages[i]
        digit = digit_of(i)
        other = lax.rem(digit + k, radix)
        return other, {axis: spot[axis] + (other - digit) * stride}

    def scatter_copy(i, k):
        held = stages[i][3]
        other, device = peer_of(i, k)
        at = other * held if accs[i].shape[0] != held else 0
        return pltpu.make_async_remote_copy(
            src_ref=accs[i].at[pl.ds(pl.multiple_of(at, 16), held)],
            dst_ref=recvs[i].at[k - 1],
            send_sem=rs_send[i].at[k - 1], recv_sem=rs_recv[i].at[k - 1],
            device_id=device, device_id_type=MESH,
        )

    def step(c, carry):
        lanes = pl.ds(pl.multiple_of(c * LANES, LANES), LANES)
        queries = (both_heads(q_ref[:, lanes]) * scaling).astype(jnp.bfloat16)
        grads = both_heads(u_ref[:, lanes]).astype(jnp.bfloat16)
        for b in order:
            if b:
                kv_copy(c, b).wait_recv()

        @pl.when(c > 0)
        def _():
            kv_copy(c, 0).wait_recv()

        @pl.when(has_edge)
        def _():
            kv_edge(c).wait_recv()

        @pl.when(c + ahead < chunks)
        def _():
            send_kv(c + ahead)

        keys = kv[c, 0]
        values = kv[c, 1]
        scores = dot(keys, queries, NT) + bias[...]
        weights = jnp.exp(scores - jnp.max(scores, axis=0, keepdims=True))
        probs = weights * (1.0 / jnp.sum(weights, axis=0, keepdims=True))
        low = probs.astype(jnp.bfloat16)
        dprobs = dot(values, grads, NT)
        inner = jnp.sum(probs * dprobs, axis=0, keepdims=True)
        dscores = (probs * (dprobs - inner)).astype(jnp.bfloat16)
        pairs = ((dscores, queries), (low, grads))
        for which, (left, right) in enumerate(pairs):
            accs[0][
                pl.ds(pl.multiple_of((c * 2 + which) * globals_, globals_), globals_)
            ] = dot(left[glob_at : glob_at + globals_], right, NN).astype(jnp.bfloat16)
        for k in range(1, stages[0][2]):
            held = stages[0][3]
            ready = lax.div((peer_of(0, k)[0] + 1) * held - 1, 2 * globals_)
            if accs[0].shape[0] == held:
                ready = chunks - 1

            @pl.when(c == ready)
            def _(k=k):
                scatter_copy(0, k).start()

        for which, (left, right) in enumerate(pairs):
            made = dot(left[:glob_at], right, NN)
            own[c, which] = made[0:rows]
            terms[c, which] = made[rows:].astype(jnp.bfloat16)

        @pl.when(c < chunks - 1)
        def _():
            send_terms(c)

        att_ref[:, lanes] = by_query(dot(values, low, TN)).astype(jnp.bfloat16)
        dq_ref[:, lanes] = (by_query(dot(keys, dscores, TN)) * scaling).astype(jnp.bfloat16)
        return carry

    kv_copy(0, 0).wait_recv()
    for c in range(1, ahead):
        send_kv(c)
    lax.fori_loop(0, chunks, step, 0)
    out_copies = [
        pltpu.make_async_copy(ref, out, out_sem.at[i])
        for i, (ref, out) in enumerate(
            zip((att_ref, dq_ref, dk_ref, dv_ref, dgk_ref, dgv_ref), outs_hbm)
        )
    ]
    out_copies[0].start()
    out_copies[1].start()

    starts = []
    start = 0
    for i, (axis, stride, radix, held) in enumerate(stages):
        if accs[i].shape[0] != held:
            start = start + digit_of(i) * held
        starts.append(start)

    def scatter_start(i):
        for k in range(1, stages[i][2]):
            scatter_copy(i, k).start()

    def scatter_end(i):
        held = stages[i][3]
        at = digit_of(i) * held if accs[i].shape[0] != held else 0
        summed = accs[i][pl.ds(pl.multiple_of(at, 16), held)].astype(jnp.float32)
        for k in range(1, stages[i][2]):
            scatter_copy(i, k).wait_recv()
            summed = summed + recvs[i][k - 1].astype(jnp.float32)
        summed = summed.astype(jnp.bfloat16)
        if i + 1 < count:
            accs[i + 1][...] = summed
        else:
            final[pl.ds(pl.multiple_of(starts[i], 16), held)] = summed

    def gather_copy(i, k, at):
        held = stages[i][3]
        part = final.at[pl.ds(pl.multiple_of(at, 16), held)]
        return pltpu.make_async_remote_copy(
            src_ref=part, dst_ref=part,
            send_sem=ag_send[i].at[k - 1], recv_sem=ag_recv[i].at[k - 1],
            device_id=peer_of(i, k)[1], device_id_type=MESH,
        )

    def gather_start(i):
        for k in range(1, stages[i][2]):
            gather_copy(i, k, starts[i]).start()

    def gather_end(i):
        _, _, radix, held = stages[i]
        for k in range(1, radix):
            behind = lax.rem(digit_of(i) + radix - k, radix)
            gather_copy(i, k, starts[i] + (behind - digit_of(i)) * held).wait_recv()

    def collect(c):
        lanes = slice(c * LANES, (c + 1) * LANES)
        for b in order:
            term_copy(c, b).wait_recv()

        @pl.when(has_edge)
        def _():
            term_edge(c).wait_recv()

        low_rows = lax.broadcasted_iota(jnp.int32, (rows, LANES), 0)
        at_edge = jnp.logical_and(low_rows >= edge_first, low_rows < edge_first + BLOCK)
        for which, out in enumerate((dk_ref, dv_ref)):
            summed = own[c, which]
            for b in range(bits):
                summed = summed + back[c, which, rows * b : rows * (b + 1)].astype(jnp.float32)
            edge = back[c, which, rows * bits : rows * bits + BLOCK].astype(jnp.float32)
            edge = jnp.concatenate([edge] * blocks, axis=0)
            summed = summed + jnp.where(at_edge, edge, 0.0)
            out[:, lanes] = summed.astype(jnp.bfloat16)

    todo = list(range(chunks))
    for i in range(count):
        if i:
            scatter_start(i)
        if i and i == count - 1 and todo:
            collect(todo.pop(0))
        scatter_end(i)
    split = [i for i in range(count) if accs[i].shape[0] != stages[i][3]]
    for i in split[::-1]:
        gather_start(i)
        if i == split[-1]:
            send_terms(chunks - 1)
        if len(todo) > 1:
            collect(todo.pop(0))
        gather_end(i)
    for c in range(chunks):
        lanes = slice(c * LANES, (c + 1) * LANES)
        for which, out in enumerate((dgk_ref, dgv_ref)):
            at = (c * 2 + which) * globals_
            out[:, lanes] = final[at : at + globals_].astype(jnp.float32)
    out_copies[4].start()
    out_copies[5].start()
    for c in todo:
        collect(c)
    out_copies[2].start()
    out_copies[3].start()

    for c in range(chunks):
        for b in order:
            kv_copy(c, b).wait_send()
            term_copy(c, b).wait_send()

        @pl.when(has_edge)
        def _():
            kv_edge(c).wait_send()
            term_edge(c).wait_send()

    for i in range(count):
        for k in range(1, stages[i][2]):
            scatter_copy(i, k).wait_send()
            if i in split:
                gather_copy(i, k, starts[i]).wait_send()

    for copy in out_copies:
        copy.wait()


def write_out(*refs):
    count = len(refs) // 3
    sem = refs[-1]
    loads = [
        pltpu.make_async_copy(refs[i], refs[2 * count + i], sem.at[0, i]) for i in range(count)
    ]
    stores = [
        pltpu.make_async_copy(refs[2 * count + i], refs[count + i], sem.at[1, i])
        for i in range(count)
    ]
    for copy in loads:
        copy.start()
    for load, store in zip(loads, stores):
        load.wait()
        store.start()
    for copy in stores:
        copy.wait()


def body(shards, replicas, queries, keys, values, global_keys, global_values, upstream, ps, pb):
    _, rows, width = queries.shape
    globals_ = global_keys.shape[0]
    bits = shards.bit_length() - 1
    chunks = width // LANES
    used = rows * (1 + bits) + BLOCK + globals_
    total = -(-used // LANES) * LANES
    gathered = 2 * chunks * globals_
    stages = reduce_stages((("dp", replicas), ("ctx", shards)), gathered)
    low = jnp.bfloat16
    accs, recvs, sems = [], [], []
    held = gathered
    for _, _, radix, after in stages:
        accs.append(pltpu.VMEM((held, LANES), low))
        recvs.append(pltpu.VMEM((radix - 1, after, LANES), low))
        sems.append(pltpu.SemaphoreType.DMA((radix - 1,)))
        held = after
    hbm = pl.BlockSpec(memory_space=pltpu.HBM)
    dma = pltpu.SemaphoreType.DMA((chunks, bits + 1))
    remote = rows * bits + BLOCK
    results = [((rows, width), low)] * 4 + [((globals_, width), jnp.float32)] * 2
    outs = pl.pallas_call(
        functools.partial(kernel, shards, stages),
        out_shape=[jax.ShapeDtypeStruct(*x) for x in results],
        in_specs=[hbm] * 8,
        out_specs=[hbm] * 6,
        scratch_shapes=[
            *[pltpu.VMEM(*x) for x in results],
            pltpu.SemaphoreType.DMA((6,)),
            pltpu.VMEM((rows, width), low),
            pltpu.VMEM((rows, width), low),
            pltpu.SMEM(ps.T.shape, jnp.int32),
            pltpu.SMEM(pb.T.shape, jnp.int32),
            pltpu.SemaphoreType.DMA((4,)),
            pltpu.SemaphoreType.DMA((2, chunks, 2)),
            pltpu.VMEM((chunks, 2, total, LANES), low),
            pltpu.VMEM((total, 2 * rows), jnp.float32),
            pltpu.VMEM((chunks, 2, remote, LANES), low),
            pltpu.VMEM((chunks, 2, remote, LANES), low),
            pltpu.VMEM((chunks, 2, rows, LANES), jnp.float32),
            *accs,
            *recvs,
            pltpu.VMEM((gathered, LANES), low),
            dma, dma, dma, dma,
            *sems, *sems, *sems, *sems,
        ],
        compiler_params=pltpu.CompilerParams(
            collective_id=0, has_side_effects=True, vmem_limit_bytes=VMEM_BYTES
        ),
    )(queries[0], keys[0], values[0], global_keys, global_values, upstream[0], ps.T, pb.T)
    outs = pl.pallas_call(
        write_out,
        out_shape=[jax.ShapeDtypeStruct(x.shape, x.dtype) for x in outs],
        in_specs=[hbm] * 6,
        out_specs=[hbm] * 6,
        scratch_shapes=[
            *[pltpu.VMEM(*x) for x in results],
            pltpu.SemaphoreType.DMA((2, 6)),
        ],
        compiler_params=pltpu.CompilerParams(vmem_limit_bytes=VMEM_BYTES),
    )(*outs)
    return (outs[0][None], outs[1][None], outs[2][None], outs[3][None], outs[4], outs[5])


def solution(mesh):
    split = P("dp", "ctx", None)
    return jax.shard_map(
        functools.partial(body, mesh.shape["ctx"], mesh.shape["dp"]),
        mesh=mesh,
        in_specs=(split, split, split, P(), P(), split, P(), P()),
        out_specs=(split, split, split, split, P(), P()),
        check_vma=False,
    )
```

```python
import functools
import math

import jax
import jax.numpy as jnp
from jax import lax
from jax.experimental import pallas as pl
from jax.experimental.pallas import tpu as pltpu
from jax.sharding import PartitionSpec as P

HEAD_DIM = 64
BLOCK = 64
R = 3
LANES = 128
VMEM_BYTES = 63 * 1024 * 1024
MASKED = -1e30
MESH = pl.DeviceIdType.MESH
NT = (((1,), (1,)), ((), ()))
TN = (((0,), (0,)), ((), ()))


def reduce_stages(sizes, rows):
    stages = []
    for axis, size in sizes:
        stride = 1
        while stride < size:
            radix = min(8, size // stride)
            if rows % (radix * 16) == 0:
                rows //= radix
            stages.append((axis, stride, radix, rows))
            stride *= radix
    return stages


def kernel(
    shards, stages, q_hbm, k_hbm, v_hbm, gk_hbm, gv_hbm, u_hbm, ps_hbm, pb_hbm,
    *refs,
):
    outs_hbm, (att_ref, dq_ref, dk_ref, dv_ref, dgk_ref, dgv_ref) = refs[:6], refs[6:12]
    run(
        shards, stages, q_hbm, k_hbm, v_hbm, gk_hbm, gv_hbm, u_hbm, ps_hbm, pb_hbm, outs_hbm,
        att_ref, dq_ref, dk_ref, dv_ref, dgk_ref, dgv_ref, *refs[12:],
    )


def run(
    shards, stages, q_hbm, k_hbm, v_hbm, gk_hbm, gv_hbm, u_hbm, ps_hbm, pb_hbm, outs_hbm,
    att_ref, dq_ref, dk_ref, dv_ref, dgk_ref, dgv_ref, out_sem,
    q_ref, u_ref, ps_ref, pb_ref, in_sem, own_sem, kv, bias, terms, back, own, *rest,
):
    count = len(stages)
    accs, recvs = rest[:count], rest[count : 2 * count]
    final = rest[2 * count]
    kv_send, kv_recv, t_send, t_recv = rest[2 * count + 1 : 2 * count + 5]
    sems = rest[2 * count + 5 :]
    rs_send, rs_recv = sems[:count], sems[count : 2 * count]
    ag_send, ag_recv = sems[2 * count : 3 * count], sems[3 * count :]

    rows, width = q_hbm.shape
    blocks = rows // BLOCK
    chunks = width // LANES
    bits = shards.bit_length() - 1
    globals_ = gk_hbm.shape[0]
    edge_at = rows * (1 + bits)
    glob_at = edge_at + BLOCK
    total = kv.shape[2]
    me = lax.axis_index("ctx")
    spot = {"ctx": me, "dp": lax.axis_index("dp")}
    odd = lax.rem(me, 2)
    edge_peer = me - 1 + 2 * odd
    has_edge = jnp.logical_and(edge_peer >= 0, edge_peer < shards)
    edge_first = pl.multiple_of(odd * (rows - BLOCK), BLOCK)
    peers = [me + (1 << b) * (1 - 2 * lax.rem(lax.div(me, 1 << b), 2)) for b in range(bits)]

    barrier = pltpu.get_barrier_semaphore()

    def greet(axis, to):
        pl.semaphore_signal(barrier, inc=1, device_id={axis: to}, device_id_type=MESH)

    greeted = 0
    for axis, stride, radix, _ in stages:
        digit = lax.rem(lax.div(spot[axis], stride), radix)
        for k in range(1, radix):
            greet(axis, spot[axis] + (lax.rem(digit + k, radix) - digit) * stride)
            greeted += 1

    apart = all(radix < shards for axis, _, radix, _ in stages if axis == "ctx")
    if apart:

        @pl.when(has_edge)
        def _():
            greet("ctx", edge_peer)

    own_copies, in_copies = [], []
    for c in range(chunks):
        lanes = pl.ds(c * LANES, LANES)
        for which, (part, shared) in enumerate(((k_hbm, gk_hbm), (v_hbm, gv_hbm))):
            own_copies.append(
                pltpu.make_async_copy(
                    part.at[:, lanes], kv.at[c, which, pl.ds(0, rows)], own_sem.at[0, c, which]
                )
            )
            in_copies.append(
                pltpu.make_async_copy(
                    shared.at[:, lanes],
                    kv.at[c, which, pl.ds(glob_at, globals_)],
                    own_sem.at[1, c, which],
                )
            )
    for i, (src, dst) in enumerate(
        ((ps_hbm, ps_ref), (pb_hbm, pb_ref), (q_hbm, q_ref), (u_hbm, u_ref))
    ):
        in_copies.append(pltpu.make_async_copy(src, dst, in_sem.at[i]))
    for copy in own_copies + in_copies:
        copy.start()
    for copy in own_copies:
        copy.wait()

    pl.semaphore_wait(barrier, greeted + jnp.where(has_edge, 1, 0) if apart else greeted)

    def kv_copy(c, b):
        return pltpu.make_async_remote_copy(
            src_ref=kv.at[c, :, pl.ds(0, rows)],
            dst_ref=kv.at[c, :, pl.ds(rows * (1 + b), rows)],
            send_sem=kv_send.at[c, b], recv_sem=kv_recv.at[c, b],
            device_id={"ctx": peers[b]}, device_id_type=MESH,
        )

    def kv_edge(c):
        return pltpu.make_async_remote_copy(
            src_ref=kv.at[c, :, pl.ds(edge_first, BLOCK)],
            dst_ref=kv.at[c, :, pl.ds(edge_at, BLOCK)],
            send_sem=kv_send.at[c, bits], recv_sem=kv_recv.at[c, bits],
            device_id={"ctx": edge_peer}, device_id_type=MESH,
        )

    def term_copy(c, b):
        return pltpu.make_async_remote_copy(
            src_ref=terms.at[c, :, pl.ds(rows * b, rows)],
            dst_ref=back.at[c, :, pl.ds(rows * b, rows)],
            send_sem=t_send.at[c, b], recv_sem=t_recv.at[c, b],
            device_id={"ctx": peers[b]}, device_id_type=MESH,
        )

    def term_edge(c):
        return pltpu.make_async_remote_copy(
            src_ref=terms.at[c, :, pl.ds(rows * bits, BLOCK)],
            dst_ref=back.at[c, :, pl.ds(rows * bits, BLOCK)],
            send_sem=t_send.at[c, bits], recv_sem=t_recv.at[c, bits],
            device_id={"ctx": edge_peer}, device_id_type=MESH,
        )

    order = list(range(bits))[::-1]

    def send_kv(c):
        for b in order:
            kv_copy(c, b).start()

        @pl.when(has_edge)
        def _():
            kv_edge(c).start()

    def send_terms(c):
        for b in order:
            term_copy(c, b).start()

        @pl.when(has_edge)
        def _():
            term_edge(c).start()

    ahead = min(2, chunks)
    for c in range(ahead):
        send_kv(c)

    for copy in in_copies:
        copy.wait()
    for c in range(chunks):
        if total > glob_at + globals_:
            kv[c, :, glob_at + globals_ :] = jnp.zeros(
                (2, total - glob_at - globals_, LANES), kv.dtype
            )

    @pl.when(jnp.logical_not(has_edge))
    def _():
        kv[:, :, edge_at : edge_at + BLOCK] = jnp.zeros((chunks, 2, BLOCK, LANES), kv.dtype)
        back[:, :, rows * bits : rows * bits + BLOCK] = jnp.zeros(
            (chunks, 2, BLOCK, LANES), back.dtype
        )

    pair = 2 * rows
    query_block = lax.rem(lax.div(lax.broadcasted_iota(jnp.int32, (8, pair), 1), BLOCK), blocks)
    first_block = me * blocks
    listed = [
        [(ps_ref[r, first_block + n], pb_ref[r, first_block + n]) for r in range(R)]
        for n in range(blocks)
    ]

    def put_bias(at, counts):
        times = jnp.zeros((8, pair), jnp.int32)
        for n in range(blocks):
            times = jnp.where(query_block == n, counts[n], times)
        times = times.astype(jnp.float32)
        line = jnp.where(times > 0.5, jnp.log(jnp.maximum(times, 1.0)), MASKED)
        for step in range(BLOCK // 8):
            bias[at + step * 8 : at + step * 8 + 8] = line

    for j in range(blocks):
        put_bias(j * BLOCK, [jnp.int32(1 if abs(j - n) <= 1 else 0) for n in range(blocks)])
    for b in range(bits):
        for j in range(blocks):
            counts = []
            for n in range(blocks):
                times = jnp.int32(0)
                for shard, block in listed[n]:
                    times += jnp.where(shard == peers[b], 1, 0) * jnp.where(block == j, 1, 0)
                if b == 0 and j == 0 and n == blocks - 1:
                    times += 1 - odd
                if b == 0 and j == blocks - 1 and n == 0:
                    times += odd
                counts.append(times)
            put_bias(rows * (1 + b) + j * BLOCK, counts)
    valid = jnp.where(has_edge, 1, 0)
    edge_counts = [jnp.int32(0)] * blocks
    edge_counts[0] = edge_counts[0] + (1 - odd) * valid
    edge_counts[blocks - 1] = edge_counts[blocks - 1] + odd * valid
    put_bias(edge_at, edge_counts)
    for at in range(glob_at, glob_at + globals_, BLOCK):
        put_bias(at, [jnp.int32(1)] * blocks)
    if total > glob_at + globals_:
        bias[glob_at + globals_ :] = jnp.full((total - glob_at - globals_, pair), MASKED)

    low_head = lax.broadcasted_iota(jnp.int32, (rows, LANES), 1) < HEAD_DIM
    scaling = 1.0 / math.sqrt(HEAD_DIM)

    def both_heads(x):
        x = x.astype(jnp.float32)
        zero = jnp.zeros_like(x)
        return jnp.concatenate(
            [jnp.where(low_head, x, zero), jnp.where(low_head, zero, x)], axis=0
        )

    def dot(a, b, dims):
        return lax.dot_general(a, b, dims, preferred_element_type=jnp.float32)

    NN = (((1,), (0,)), ((), ()))

    def by_query(x):
        return jnp.concatenate([x[:HEAD_DIM, :rows], x[HEAD_DIM:, rows:]], axis=0).T

    def digit_of(i):
        axis, stride, radix, _ = stages[i]
        return lax.rem(lax.div(spot[axis], stride), radix)

    def peer_of(i, k):
        axis, stride, radix, _ = stages[i]
        digit = digit_of(i)
        other = lax.rem(digit + k, radix)
        return other, {axis: spot[axis] + (other - digit) * stride}

    def scatter_copy(i, k):
        held = stages[i][3]
        other, device = peer_of(i, k)
        at = other * held if accs[i].shape[0] != held else 0
        return pltpu.make_async_remote_copy(
            src_ref=accs[i].at[pl.ds(pl.multiple_of(at, 16), held)],
            dst_ref=recvs[i].at[k - 1],
            send_sem=rs_send[i].at[k - 1], recv_sem=rs_recv[i].at[k - 1],
            device_id=device, device_id_type=MESH,
        )

    def step(c, carry):
        lanes = pl.ds(pl.multiple_of(c * LANES, LANES), LANES)
        queries = (both_heads(q_ref[:, lanes]) * scaling).astype(jnp.bfloat16)
        grads = both_heads(u_ref[:, lanes]).astype(jnp.bfloat16)
        for b in order:
            kv_copy(c, b).wait_recv()

        @pl.when(has_edge)
        def _():
            kv_edge(c).wait_recv()

        @pl.when(c + ahead < chunks)
        def _():
            send_kv(c + ahead)

        @pl.when(c == chunks - 1)
        def _():
            for done in range(chunks - 2):
                send_terms(done)

        keys = kv[c, 0]
        values = kv[c, 1]
        scores = dot(keys, queries, NT) + bias[...]
        weights = jnp.exp(scores - jnp.max(scores, axis=0, keepdims=True))
        probs = weights * (1.0 / jnp.sum(weights, axis=0, keepdims=True))
        low = probs.astype(jnp.bfloat16)
        dprobs = dot(values, grads, NT)
        inner = jnp.sum(probs * dprobs, axis=0, keepdims=True)
        dscores = (probs * (dprobs - inner)).astype(jnp.bfloat16)
        pairs = ((dscores, queries), (low, grads))
        for which, (left, right) in enumerate(pairs):
            accs[0][
                pl.ds(pl.multiple_of((c * 2 + which) * globals_, globals_), globals_)
            ] = dot(left[glob_at : glob_at + globals_], right, NN).astype(jnp.bfloat16)
        for k in range(1, stages[0][2]):
            held = stages[0][3]
            ready = lax.div((peer_of(0, k)[0] + 1) * held - 1, 2 * globals_)
            if accs[0].shape[0] == held:
                ready = chunks - 1

            @pl.when(c == ready)
            def _(k=k):
                scatter_copy(0, k).start()

        for which, (left, right) in enumerate(pairs):
            made = dot(left[:glob_at], right, NN)
            own[c, which] = made[0:rows]
            terms[c, which] = made[rows:].astype(jnp.bfloat16)

        att_ref[:, lanes] = by_query(dot(values, low, TN)).astype(jnp.bfloat16)
        dq_ref[:, lanes] = (by_query(dot(keys, dscores, TN)) * scaling).astype(jnp.bfloat16)
        return carry

    lax.fori_loop(0, chunks, step, 0)
    out_copies = [
        pltpu.make_async_copy(ref, out, out_sem.at[i])
        for i, (ref, out) in enumerate(
            zip((att_ref, dq_ref, dk_ref, dv_ref, dgk_ref, dgv_ref), outs_hbm)
        )
    ]
    out_copies[0].start()
    out_copies[1].start()

    starts = []
    start = 0
    for i, (axis, stride, radix, held) in enumerate(stages):
        if accs[i].shape[0] != held:
            start = start + digit_of(i) * held
        starts.append(start)

    def scatter_start(i):
        for k in range(1, stages[i][2]):
            scatter_copy(i, k).start()

    def scatter_end(i):
        held = stages[i][3]
        at = digit_of(i) * held if accs[i].shape[0] != held else 0
        summed = accs[i][pl.ds(pl.multiple_of(at, 16), held)].astype(jnp.float32)
        for k in range(1, stages[i][2]):
            scatter_copy(i, k).wait_recv()
            summed = summed + recvs[i][k - 1].astype(jnp.float32)
        summed = summed.astype(jnp.bfloat16)
        if i + 1 < count:
            accs[i + 1][...] = summed
        else:
            final[pl.ds(pl.multiple_of(starts[i], 16), held)] = summed

    def gather_copy(i, k, at):
        held = stages[i][3]
        part = final.at[pl.ds(pl.multiple_of(at, 16), held)]
        return pltpu.make_async_remote_copy(
            src_ref=part, dst_ref=part,
            send_sem=ag_send[i].at[k - 1], recv_sem=ag_recv[i].at[k - 1],
            device_id=peer_of(i, k)[1], device_id_type=MESH,
        )

    def gather_start(i):
        for k in range(1, stages[i][2]):
            gather_copy(i, k, starts[i]).start()

    def gather_end(i):
        _, _, radix, held = stages[i]
        for k in range(1, radix):
            behind = lax.rem(digit_of(i) + radix - k, radix)
            gather_copy(i, k, starts[i] + (behind - digit_of(i)) * held).wait_recv()

    def collect(c):
        lanes = slice(c * LANES, (c + 1) * LANES)
        for b in order:
            term_copy(c, b).wait_recv()

        @pl.when(has_edge)
        def _():
            term_edge(c).wait_recv()

        low_rows = lax.broadcasted_iota(jnp.int32, (rows, LANES), 0)
        at_edge = jnp.logical_and(low_rows >= edge_first, low_rows < edge_first + BLOCK)
        for which, out in enumerate((dk_ref, dv_ref)):
            summed = own[c, which]
            for b in range(bits):
                summed = summed + back[c, which, rows * b : rows * (b + 1)].astype(jnp.float32)
            edge = back[c, which, rows * bits : rows * bits + BLOCK].astype(jnp.float32)
            edge = jnp.concatenate([edge] * blocks, axis=0)
            summed = summed + jnp.where(at_edge, edge, 0.0)
            out[:, lanes] = summed.astype(jnp.bfloat16)

    todo = list(range(chunks))
    for i in range(count):
        if i:
            scatter_start(i)
        if i == count - 1 and chunks > 1:
            send_terms(chunks - 2)
        scatter_end(i)
    split = [i for i in range(count) if accs[i].shape[0] != stages[i][3]]
    for i in split[::-1]:
        gather_start(i)
        if i == split[-1]:
            send_terms(chunks - 1)
        if len(todo) > 1:
            collect(todo.pop(0))
        gather_end(i)
    for c in range(chunks):
        lanes = slice(c * LANES, (c + 1) * LANES)
        for which, out in enumerate((dgk_ref, dgv_ref)):
            at = (c * 2 + which) * globals_
            out[:, lanes] = final[at : at + globals_].astype(jnp.float32)
    out_copies[4].start()
    out_copies[5].start()
    for c in todo:
        collect(c)
    out_copies[2].start()
    out_copies[3].start()

    for c in range(chunks):
        for b in order:
            kv_copy(c, b).wait_send()
            term_copy(c, b).wait_send()

        @pl.when(has_edge)
        def _():
            kv_edge(c).wait_send()
            term_edge(c).wait_send()

    for i in range(count):
        for k in range(1, stages[i][2]):
            scatter_copy(i, k).wait_send()
            if i in split:
                gather_copy(i, k, starts[i]).wait_send()

    for copy in out_copies:
        copy.wait()


def write_out(*refs):
    count = len(refs) // 3
    sem = refs[-1]
    loads = [
        pltpu.make_async_copy(refs[i], refs[2 * count + i], sem.at[0, i]) for i in range(count)
    ]
    stores = [
        pltpu.make_async_copy(refs[2 * count + i], refs[count + i], sem.at[1, i])
        for i in range(count)
    ]
    for copy in loads:
        copy.start()
    for load, store in zip(loads, stores):
        load.wait()
        store.start()
    for copy in stores:
        copy.wait()


def body(shards, replicas, queries, keys, values, global_keys, global_values, upstream, ps, pb):
    _, rows, width = queries.shape
    globals_ = global_keys.shape[0]
    bits = shards.bit_length() - 1
    chunks = width // LANES
    used = rows * (1 + bits) + BLOCK + globals_
    total = -(-used // LANES) * LANES
    gathered = 2 * chunks * globals_
    stages = reduce_stages((("dp", replicas), ("ctx", shards)), gathered)
    low = jnp.bfloat16
    accs, recvs, sems = [], [], []
    held = gathered
    for _, _, radix, after in stages:
        accs.append(pltpu.VMEM((held, LANES), low))
        recvs.append(pltpu.VMEM((radix - 1, after, LANES), low))
        sems.append(pltpu.SemaphoreType.DMA((radix - 1,)))
        held = after
    hbm = pl.BlockSpec(memory_space=pltpu.HBM)
    dma = pltpu.SemaphoreType.DMA((chunks, bits + 1))
    remote = rows * bits + BLOCK
    results = [((rows, width), low)] * 4 + [((globals_, width), jnp.float32)] * 2
    outs = pl.pallas_call(
        functools.partial(kernel, shards, stages),
        out_shape=[jax.ShapeDtypeStruct(*x) for x in results],
        in_specs=[hbm] * 8,
        out_specs=[hbm] * 6,
        scratch_shapes=[
            *[pltpu.VMEM(*x) for x in results],
            pltpu.SemaphoreType.DMA((6,)),
            pltpu.VMEM((rows, width), low),
            pltpu.VMEM((rows, width), low),
            pltpu.SMEM(ps.T.shape, jnp.int32),
            pltpu.SMEM(pb.T.shape, jnp.int32),
            pltpu.SemaphoreType.DMA((4,)),
            pltpu.SemaphoreType.DMA((2, chunks, 2)),
            pltpu.VMEM((chunks, 2, total, LANES), low),
            pltpu.VMEM((total, 2 * rows), jnp.float32),
            pltpu.VMEM((chunks, 2, remote, LANES), low),
            pltpu.VMEM((chunks, 2, remote, LANES), low),
            pltpu.VMEM((chunks, 2, rows, LANES), jnp.float32),
            *accs,
            *recvs,
            pltpu.VMEM((gathered, LANES), low),
            dma, dma, dma, dma,
            *sems, *sems, *sems, *sems,
        ],
        compiler_params=pltpu.CompilerParams(
            collective_id=0, has_side_effects=True, vmem_limit_bytes=VMEM_BYTES
        ),
    )(queries[0], keys[0], values[0], global_keys, global_values, upstream[0], ps.T, pb.T)
    outs = pl.pallas_call(
        write_out,
        out_shape=[jax.ShapeDtypeStruct(x.shape, x.dtype) for x in outs],
        in_specs=[hbm] * 6,
        out_specs=[hbm] * 6,
        scratch_shapes=[
            *[pltpu.VMEM(*x) for x in results],
            pltpu.SemaphoreType.DMA((2, 6)),
        ],
        compiler_params=pltpu.CompilerParams(vmem_limit_bytes=VMEM_BYTES),
    )(*outs)
    return (outs[0][None], outs[1][None], outs[2][None], outs[3][None], outs[4], outs[5])


def solution(mesh):
    split = P("dp", "ctx", None)
    return jax.shard_map(
        functools.partial(body, mesh.shape["ctx"], mesh.shape["dp"]),
        mesh=mesh,
        in_specs=(split, split, split, P(), P(), split, P(), P()),
        out_specs=(split, split, split, split, P(), P()),
        check_vma=False,
    )
```

```python
import functools
import math

import jax
import jax.numpy as jnp
from jax import lax
from jax.experimental import pallas as pl
from jax.experimental.pallas import tpu as pltpu
from jax.sharding import PartitionSpec as P

HEAD_DIM = 64
BLOCK = 64
R = 3
LANES = 128
VMEM_BYTES = 63 * 1024 * 1024
MASKED = -1e30
MESH = pl.DeviceIdType.MESH
NT = (((1,), (1,)), ((), ()))
TN = (((0,), (0,)), ((), ()))


def reduce_stages(sizes, rows):
    stages = []
    for axis, size in sizes:
        stride = 1
        while stride < size:
            radix = min(8, size // stride)
            if rows % (radix * 16) == 0:
                rows //= radix
            stages.append((axis, stride, radix, rows))
            stride *= radix
    return stages


def kernel(
    shards, stages, q_hbm, k_hbm, v_hbm, gk_hbm, gv_hbm, u_hbm, ps_hbm, pb_hbm,
    *refs,
):
    outs_hbm, (att_ref, dq_ref, dk_ref, dv_ref, dgk_ref, dgv_ref) = refs[:6], refs[6:12]
    run(
        shards, stages, q_hbm, k_hbm, v_hbm, gk_hbm, gv_hbm, u_hbm, ps_hbm, pb_hbm, outs_hbm,
        att_ref, dq_ref, dk_ref, dv_ref, dgk_ref, dgv_ref, *refs[12:],
    )


def run(
    shards, stages, q_hbm, k_hbm, v_hbm, gk_hbm, gv_hbm, u_hbm, ps_hbm, pb_hbm, outs_hbm,
    att_ref, dq_ref, dk_ref, dv_ref, dgk_ref, dgv_ref, out_sem,
    q_ref, u_ref, ps_ref, pb_ref, in_sem, own_sem, weight_s, dprob_s, low_s, dscore_s, kv, bias, terms, back, own, *rest,
):
    count = len(stages)
    accs, recvs = rest[:count], rest[count : 2 * count]
    final = rest[2 * count]
    kv_send, kv_recv, t_send, t_recv = rest[2 * count + 1 : 2 * count + 5]
    sems = rest[2 * count + 5 :]
    rs_send, rs_recv = sems[:count], sems[count : 2 * count]
    ag_send, ag_recv = sems[2 * count : 3 * count], sems[3 * count :]

    rows, width = q_hbm.shape
    blocks = rows // BLOCK
    chunks = width // LANES
    bits = shards.bit_length() - 1
    globals_ = gk_hbm.shape[0]
    edge_at = rows * (1 + bits)
    glob_at = edge_at + BLOCK
    tiles = [(rows * i, rows) for i in range(1 + bits)] + [(edge_at, BLOCK), (glob_at, globals_)]
    me = lax.axis_index("ctx")
    spot = {"ctx": me, "dp": lax.axis_index("dp")}
    odd = lax.rem(me, 2)
    edge_peer = me - 1 + 2 * odd
    has_edge = jnp.logical_and(edge_peer >= 0, edge_peer < shards)
    edge_first = pl.multiple_of(odd * (rows - BLOCK), BLOCK)
    peers = [me + (1 << b) * (1 - 2 * lax.rem(lax.div(me, 1 << b), 2)) for b in range(bits)]

    barrier = pltpu.get_barrier_semaphore()

    def greet(axis, to):
        pl.semaphore_signal(barrier, inc=1, device_id={axis: to}, device_id_type=MESH)

    greeted = 0
    for axis, stride, radix, _ in stages:
        digit = lax.rem(lax.div(spot[axis], stride), radix)
        for k in range(1, radix):
            greet(axis, spot[axis] + (lax.rem(digit + k, radix) - digit) * stride)
            greeted += 1

    apart = all(radix < shards for axis, _, radix, _ in stages if axis == "ctx")
    if apart:

        @pl.when(has_edge)
        def _():
            greet("ctx", edge_peer)

    own_copies, in_copies = [], []
    for c in range(chunks):
        lanes = pl.ds(c * LANES, LANES)
        for which, (part, shared) in enumerate(((k_hbm, gk_hbm), (v_hbm, gv_hbm))):
            own_copies.append(
                pltpu.make_async_copy(
                    part.at[:, lanes], kv.at[c, which, pl.ds(0, rows)], own_sem.at[0, c, which]
                )
            )
            in_copies.append(
                pltpu.make_async_copy(
                    shared.at[:, lanes],
                    kv.at[c, which, pl.ds(glob_at, globals_)],
                    own_sem.at[1, c, which],
                )
            )
    for i, (src, dst) in enumerate(
        ((ps_hbm, ps_ref), (pb_hbm, pb_ref), (q_hbm, q_ref), (u_hbm, u_ref))
    ):
        in_copies.append(pltpu.make_async_copy(src, dst, in_sem.at[i]))
    for copy in own_copies + in_copies:
        copy.start()
    for copy in own_copies:
        copy.wait()

    pl.semaphore_wait(barrier, greeted + jnp.where(has_edge, 1, 0) if apart else greeted)

    def kv_copy(c, b):
        return pltpu.make_async_remote_copy(
            src_ref=kv.at[c, :, pl.ds(0, rows)],
            dst_ref=kv.at[c, :, pl.ds(rows * (1 + b), rows)],
            send_sem=kv_send.at[c, b], recv_sem=kv_recv.at[c, b],
            device_id={"ctx": peers[b]}, device_id_type=MESH,
        )

    def kv_edge(c):
        return pltpu.make_async_remote_copy(
            src_ref=kv.at[c, :, pl.ds(edge_first, BLOCK)],
            dst_ref=kv.at[c, :, pl.ds(edge_at, BLOCK)],
            send_sem=kv_send.at[c, bits], recv_sem=kv_recv.at[c, bits],
            device_id={"ctx": edge_peer}, device_id_type=MESH,
        )

    def term_copy(c, b):
        return pltpu.make_async_remote_copy(
            src_ref=terms.at[c, :, pl.ds(rows * b, rows)],
            dst_ref=back.at[c, :, pl.ds(rows * b, rows)],
            send_sem=t_send.at[c, b], recv_sem=t_recv.at[c, b],
            device_id={"ctx": peers[b]}, device_id_type=MESH,
        )

    def term_edge(c):
        return pltpu.make_async_remote_copy(
            src_ref=terms.at[c, :, pl.ds(rows * bits, BLOCK)],
            dst_ref=back.at[c, :, pl.ds(rows * bits, BLOCK)],
            send_sem=t_send.at[c, bits], recv_sem=t_recv.at[c, bits],
            device_id={"ctx": edge_peer}, device_id_type=MESH,
        )

    order = list(range(bits))[::-1]

    def send_kv(c):
        for b in order:
            kv_copy(c, b).start()

        @pl.when(has_edge)
        def _():
            kv_edge(c).start()

    def send_terms(c):
        for b in order:
            term_copy(c, b).start()

        @pl.when(has_edge)
        def _():
            term_edge(c).start()

    ahead = min(2, chunks)
    for c in range(ahead):
        send_kv(c)

    for copy in in_copies:
        copy.wait()

    @pl.when(jnp.logical_not(has_edge))
    def _():
        kv[:, :, edge_at : edge_at + BLOCK] = jnp.zeros((chunks, 2, BLOCK, LANES), kv.dtype)
        back[:, :, rows * bits : rows * bits + BLOCK] = jnp.zeros(
            (chunks, 2, BLOCK, LANES), back.dtype
        )

    pair = 2 * rows
    query_block = lax.rem(lax.div(lax.broadcasted_iota(jnp.int32, (8, pair), 1), BLOCK), blocks)
    first_block = me * blocks
    listed = [
        [(ps_ref[r, first_block + n], pb_ref[r, first_block + n]) for r in range(R)]
        for n in range(blocks)
    ]

    def put_bias(at, counts):
        times = jnp.zeros((8, pair), jnp.int32)
        for n in range(blocks):
            times = jnp.where(query_block == n, counts[n], times)
        times = times.astype(jnp.float32)
        line = jnp.where(times > 0.5, jnp.log(jnp.maximum(times, 1.0)), MASKED)
        for step in range(BLOCK // 8):
            bias[at + step * 8 : at + step * 8 + 8] = line

    for j in range(blocks):
        put_bias(j * BLOCK, [jnp.int32(1 if abs(j - n) <= 1 else 0) for n in range(blocks)])
    for b in range(bits):
        for j in range(blocks):
            counts = []
            for n in range(blocks):
                times = jnp.int32(0)
                for shard, block in listed[n]:
                    times += jnp.where(shard == peers[b], 1, 0) * jnp.where(block == j, 1, 0)
                if b == 0 and j == 0 and n == blocks - 1:
                    times += 1 - odd
                if b == 0 and j == blocks - 1 and n == 0:
                    times += odd
                counts.append(times)
            put_bias(rows * (1 + b) + j * BLOCK, counts)
    valid = jnp.where(has_edge, 1, 0)
    edge_counts = [jnp.int32(0)] * blocks
    edge_counts[0] = edge_counts[0] + (1 - odd) * valid
    edge_counts[blocks - 1] = edge_counts[blocks - 1] + odd * valid
    put_bias(edge_at, edge_counts)
    for at in range(glob_at, glob_at + globals_, BLOCK):
        put_bias(at, [jnp.int32(1)] * blocks)

    low_head = lax.broadcasted_iota(jnp.int32, (rows, LANES), 1) < HEAD_DIM
    scaling = 1.0 / math.sqrt(HEAD_DIM)

    def both_heads(x):
        x = x.astype(jnp.float32)
        zero = jnp.zeros_like(x)
        return jnp.concatenate(
            [jnp.where(low_head, x, zero), jnp.where(low_head, zero, x)], axis=0
        )

    def dot(a, b, dims):
        return lax.dot_general(a, b, dims, preferred_element_type=jnp.float32)

    NN = (((1,), (0,)), ((), ()))

    def by_query(x):
        return jnp.concatenate([x[:HEAD_DIM, :rows], x[HEAD_DIM:, rows:]], axis=0).T

    def digit_of(i):
        axis, stride, radix, _ = stages[i]
        return lax.rem(lax.div(spot[axis], stride), radix)

    def peer_of(i, k):
        axis, stride, radix, _ = stages[i]
        digit = digit_of(i)
        other = lax.rem(digit + k, radix)
        return other, {axis: spot[axis] + (other - digit) * stride}

    def scatter_copy(i, k):
        held = stages[i][3]
        other, device = peer_of(i, k)
        at = other * held if accs[i].shape[0] != held else 0
        return pltpu.make_async_remote_copy(
            src_ref=accs[i].at[pl.ds(pl.multiple_of(at, 16), held)],
            dst_ref=recvs[i].at[k - 1],
            send_sem=rs_send[i].at[k - 1], recv_sem=rs_recv[i].at[k - 1],
            device_id=device, device_id_type=MESH,
        )

    def step(c, carry):
        lanes = pl.ds(pl.multiple_of(c * LANES, LANES), LANES)
        queries = (both_heads(q_ref[:, lanes]) * scaling).astype(jnp.bfloat16)
        grads = both_heads(u_ref[:, lanes]).astype(jnp.bfloat16)
        for b in order:
            kv_copy(c, b).wait_recv()

        @pl.when(has_edge)
        def _():
            kv_edge(c).wait_recv()

        @pl.when(c + ahead < chunks)
        def _():
            send_kv(c + ahead)

        @pl.when(c == chunks - 1)
        def _():
            for done in range(chunks - 2):
                send_terms(done)

        top = None
        for at, size in tiles:
            rows_at = slice(at, at + size)
            scores = dot(kv[c, 0, rows_at], queries, NT) + bias[rows_at]
            weight_s[rows_at] = scores
            part = jnp.max(scores, axis=0, keepdims=True)
            top = part if top is None else jnp.maximum(top, part)
        norm = mixed = jnp.zeros((1, pair), jnp.float32)
        for at, size in tiles:
            rows_at = slice(at, at + size)
            weights = jnp.exp(weight_s[rows_at] - top)
            dprobs = dot(kv[c, 1, rows_at], grads, NT)
            weight_s[rows_at] = weights
            dprob_s[rows_at] = dprobs
            norm = norm + jnp.sum(weights, axis=0, keepdims=True)
            mixed = mixed + jnp.sum(weights * dprobs, axis=0, keepdims=True)
        inverse = 1.0 / norm
        inner = mixed * inverse

        def products(at, size):
            rows_at = slice(at, at + size)
            probs = weight_s[rows_at] * inverse
            low = probs.astype(jnp.bfloat16)
            dscores = (probs * (dprob_s[rows_at] - inner)).astype(jnp.bfloat16)
            low_s[rows_at] = low
            dscore_s[rows_at] = dscores
            return dot(dscores, queries, NN), dot(low, grads, NN)

        for which, made in enumerate(products(*tiles[-1])):
            accs[0][
                pl.ds(pl.multiple_of((c * 2 + which) * globals_, globals_), globals_)
            ] = made.astype(jnp.bfloat16)
        for k in range(1, stages[0][2]):
            held = stages[0][3]
            ready = lax.div((peer_of(0, k)[0] + 1) * held - 1, 2 * globals_)
            if accs[0].shape[0] == held:
                ready = chunks - 1

            @pl.when(c == ready)
            def _(k=k):
                scatter_copy(0, k).start()

        for at, size in tiles[1:-1]:
            for which, made in enumerate(products(at, size)):
                terms[c, which, at - rows : at - rows + size] = made.astype(jnp.bfloat16)
        for which, made in enumerate(products(*tiles[0])):
            own[c, which] = made
        att_ref[:, lanes] = by_query(dot(kv[c, 1], low_s[...], TN)).astype(jnp.bfloat16)
        dq_ref[:, lanes] = (by_query(dot(kv[c, 0], dscore_s[...], TN)) * scaling).astype(
            jnp.bfloat16
        )
        return carry

    lax.fori_loop(0, chunks, step, 0)
    out_copies = [
        pltpu.make_async_copy(ref, out, out_sem.at[i])
        for i, (ref, out) in enumerate(
            zip((att_ref, dq_ref, dk_ref, dv_ref, dgk_ref, dgv_ref), outs_hbm)
        )
    ]
    out_copies[0].start()
    out_copies[1].start()

    starts = []
    start = 0
    for i, (axis, stride, radix, held) in enumerate(stages):
        if accs[i].shape[0] != held:
            start = start + digit_of(i) * held
        starts.append(start)

    def scatter_start(i):
        for k in range(1, stages[i][2]):
            scatter_copy(i, k).start()

    def scatter_end(i):
        held = stages[i][3]
        at = digit_of(i) * held if accs[i].shape[0] != held else 0
        summed = accs[i][pl.ds(pl.multiple_of(at, 16), held)].astype(jnp.float32)
        for k in range(1, stages[i][2]):
            scatter_copy(i, k).wait_recv()
            summed = summed + recvs[i][k - 1].astype(jnp.float32)
        summed = summed.astype(jnp.bfloat16)
        if i + 1 < count:
            accs[i + 1][...] = summed
        else:
            final[pl.ds(pl.multiple_of(starts[i], 16), held)] = summed

    def gather_copy(i, k, at):
        held = stages[i][3]
        part = final.at[pl.ds(pl.multiple_of(at, 16), held)]
        return pltpu.make_async_remote_copy(
            src_ref=part, dst_ref=part,
            send_sem=ag_send[i].at[k - 1], recv_sem=ag_recv[i].at[k - 1],
            device_id=peer_of(i, k)[1], device_id_type=MESH,
        )

    def gather_start(i):
        for k in range(1, stages[i][2]):
            gather_copy(i, k, starts[i]).start()

    def gather_end(i):
        _, _, radix, held = stages[i]
        for k in range(1, radix):
            behind = lax.rem(digit_of(i) + radix - k, radix)
            gather_copy(i, k, starts[i] + (behind - digit_of(i)) * held).wait_recv()

    def collect(c):
        lanes = slice(c * LANES, (c + 1) * LANES)
        for b in order:
            term_copy(c, b).wait_recv()

        @pl.when(has_edge)
        def _():
            term_edge(c).wait_recv()

        low_rows = lax.broadcasted_iota(jnp.int32, (rows, LANES), 0)
        at_edge = jnp.logical_and(low_rows >= edge_first, low_rows < edge_first + BLOCK)
        for which, out in enumerate((dk_ref, dv_ref)):
            summed = own[c, which]
            for b in range(bits):
                summed = summed + back[c, which, rows * b : rows * (b + 1)].astype(jnp.float32)
            edge = back[c, which, rows * bits : rows * bits + BLOCK].astype(jnp.float32)
            edge = jnp.concatenate([edge] * blocks, axis=0)
            summed = summed + jnp.where(at_edge, edge, 0.0)
            out[:, lanes] = summed.astype(jnp.bfloat16)

    todo = list(range(chunks))
    for i in range(count):
        if i:
            scatter_start(i)
        if i == count - 1 and chunks > 1:
            send_terms(chunks - 2)
        scatter_end(i)
    split = [i for i in range(count) if accs[i].shape[0] != stages[i][3]]
    for i in split[::-1]:
        gather_start(i)
        if i == split[-1]:
            send_terms(chunks - 1)
        if len(todo) > 1:
            collect(todo.pop(0))
        gather_end(i)
    for c in range(chunks):
        lanes = slice(c * LANES, (c + 1) * LANES)
        for which, out in enumerate((dgk_ref, dgv_ref)):
            at = (c * 2 + which) * globals_
            out[:, lanes] = final[at : at + globals_].astype(jnp.float32)
    out_copies[4].start()
    out_copies[5].start()
    for c in todo:
        collect(c)
    out_copies[2].start()
    out_copies[3].start()

    for c in range(chunks):
        for b in order:
            kv_copy(c, b).wait_send()
            term_copy(c, b).wait_send()

        @pl.when(has_edge)
        def _():
            kv_edge(c).wait_send()
            term_edge(c).wait_send()

    for i in range(count):
        for k in range(1, stages[i][2]):
            scatter_copy(i, k).wait_send()
            if i in split:
                gather_copy(i, k, starts[i]).wait_send()

    for copy in out_copies:
        copy.wait()


def write_out(*refs):
    count = len(refs) // 3
    sem = refs[-1]
    loads = [
        pltpu.make_async_copy(refs[i], refs[2 * count + i], sem.at[0, i]) for i in range(count)
    ]
    stores = [
        pltpu.make_async_copy(refs[2 * count + i], refs[count + i], sem.at[1, i])
        for i in range(count)
    ]
    for copy in loads:
        copy.start()
    for load, store in zip(loads, stores):
        load.wait()
        store.start()
    for copy in stores:
        copy.wait()


def body(shards, replicas, queries, keys, values, global_keys, global_values, upstream, ps, pb):
    _, rows, width = queries.shape
    globals_ = global_keys.shape[0]
    bits = shards.bit_length() - 1
    chunks = width // LANES
    total = rows * (1 + bits) + BLOCK + globals_
    gathered = 2 * chunks * globals_
    stages = reduce_stages((("dp", replicas), ("ctx", shards)), gathered)
    low = jnp.bfloat16
    accs, recvs, sems = [], [], []
    held = gathered
    for _, _, radix, after in stages:
        accs.append(pltpu.VMEM((held, LANES), low))
        recvs.append(pltpu.VMEM((radix - 1, after, LANES), low))
        sems.append(pltpu.SemaphoreType.DMA((radix - 1,)))
        held = after
    hbm = pl.BlockSpec(memory_space=pltpu.HBM)
    dma = pltpu.SemaphoreType.DMA((chunks, bits + 1))
    remote = rows * bits + BLOCK
    results = [((rows, width), low)] * 4 + [((globals_, width), jnp.float32)] * 2
    outs = pl.pallas_call(
        functools.partial(kernel, shards, stages),
        out_shape=[jax.ShapeDtypeStruct(*x) for x in results],
        in_specs=[hbm] * 8,
        out_specs=[hbm] * 6,
        scratch_shapes=[
            *[pltpu.VMEM(*x) for x in results],
            pltpu.SemaphoreType.DMA((6,)),
            pltpu.VMEM((rows, width), low),
            pltpu.VMEM((rows, width), low),
            pltpu.SMEM(ps.T.shape, jnp.int32),
            pltpu.SMEM(pb.T.shape, jnp.int32),
            pltpu.SemaphoreType.DMA((4,)),
            pltpu.SemaphoreType.DMA((2, chunks, 2)),
            *[pltpu.VMEM((total, 2 * rows), x) for x in (jnp.float32, jnp.float32, low, low)],
            pltpu.VMEM((chunks, 2, total, LANES), low),
            pltpu.VMEM((total, 2 * rows), jnp.float32),
            pltpu.VMEM((chunks, 2, remote, LANES), low),
            pltpu.VMEM((chunks, 2, remote, LANES), low),
            pltpu.VMEM((chunks, 2, rows, LANES), jnp.float32),
            *accs,
            *recvs,
            pltpu.VMEM((gathered, LANES), low),
            dma, dma, dma, dma,
            *sems, *sems, *sems, *sems,
        ],
        compiler_params=pltpu.CompilerParams(
            collective_id=0, has_side_effects=True, vmem_limit_bytes=VMEM_BYTES
        ),
    )(queries[0], keys[0], values[0], global_keys, global_values, upstream[0], ps.T, pb.T)
    outs = pl.pallas_call(
        write_out,
        out_shape=[jax.ShapeDtypeStruct(x.shape, x.dtype) for x in outs],
        in_specs=[hbm] * 6,
        out_specs=[hbm] * 6,
        scratch_shapes=[
            *[pltpu.VMEM(*x) for x in results],
            pltpu.SemaphoreType.DMA((2, 6)),
        ],
        compiler_params=pltpu.CompilerParams(vmem_limit_bytes=VMEM_BYTES),
    )(*outs)
    return (outs[0][None], outs[1][None], outs[2][None], outs[3][None], outs[4], outs[5])


def solution(mesh):
    split = P("dp", "ctx", None)
    return jax.shard_map(
        functools.partial(body, mesh.shape["ctx"], mesh.shape["dp"]),
        mesh=mesh,
        in_specs=(split, split, split, P(), P(), split, P(), P()),
        out_specs=(split, split, split, split, P(), P()),
        check_vma=False,
    )
```

```python
import functools
import math

import jax
import jax.numpy as jnp
from jax import lax
from jax.experimental import pallas as pl
from jax.experimental.pallas import tpu as pltpu
from jax.sharding import PartitionSpec as P

HEAD_DIM = 64
BLOCK = 64
R = 3
LANES = 128
VMEM_BYTES = 63 * 1024 * 1024
MASKED = -1e30
MESH = pl.DeviceIdType.MESH
NT = (((1,), (1,)), ((), ()))
TN = (((0,), (0,)), ((), ()))


def reduce_stages(sizes, rows):
    stages = []
    for axis, size in sizes:
        stride = 1
        while stride < size:
            radix = min(8, size // stride)
            if rows % (radix * 16) == 0:
                rows //= radix
            stages.append((axis, stride, radix, rows))
            stride *= radix
    return stages


def kernel(
    shards, stages, q_hbm, k_hbm, v_hbm, gk_hbm, gv_hbm, u_hbm, ps_hbm, pb_hbm,
    *refs,
):
    outs_hbm, (att_ref, dq_ref, dk_ref, dv_ref, dgk_ref, dgv_ref) = refs[:6], refs[6:12]
    run(
        shards, stages, q_hbm, k_hbm, v_hbm, gk_hbm, gv_hbm, u_hbm, ps_hbm, pb_hbm, outs_hbm,
        att_ref, dq_ref, dk_ref, dv_ref, dgk_ref, dgv_ref, *refs[12:],
    )


def run(
    shards, stages, q_hbm, k_hbm, v_hbm, gk_hbm, gv_hbm, u_hbm, ps_hbm, pb_hbm, outs_hbm,
    att_ref, dq_ref, dk_ref, dv_ref, dgk_ref, dgv_ref, out_sem,
    q_ref, u_ref, ps_ref, pb_ref, in_sem, own_sem, weight_s, dprob_s, low_s, dscore_s, kv, bias, terms, back, own, *rest,
):
    count = len(stages)
    accs, recvs = rest[:count], rest[count : 2 * count]
    final = rest[2 * count]
    kv_send, kv_recv, t_send, t_recv = rest[2 * count + 1 : 2 * count + 5]
    sems = rest[2 * count + 5 :]
    rs_send, rs_recv = sems[:count], sems[count : 2 * count]
    ag_send, ag_recv = sems[2 * count : 3 * count], sems[3 * count :]

    rows, width = q_hbm.shape
    blocks = rows // BLOCK
    chunks = width // LANES
    bits = shards.bit_length() - 1
    globals_ = gk_hbm.shape[0]
    edge_at = rows * (1 + bits)
    glob_at = edge_at + BLOCK
    tiles = [(rows * i, rows) for i in range(1 + bits)] + [(edge_at, BLOCK), (glob_at, globals_)]
    me = lax.axis_index("ctx")
    spot = {"ctx": me, "dp": lax.axis_index("dp")}
    odd = lax.rem(me, 2)
    edge_peer = me - 1 + 2 * odd
    has_edge = jnp.logical_and(edge_peer >= 0, edge_peer < shards)
    edge_first = pl.multiple_of(odd * (rows - BLOCK), BLOCK)
    peers = [me + (1 << b) * (1 - 2 * lax.rem(lax.div(me, 1 << b), 2)) for b in range(bits)]

    barrier = pltpu.get_barrier_semaphore()

    def greet(axis, to):
        pl.semaphore_signal(barrier, inc=1, device_id={axis: to}, device_id_type=MESH)

    greeted = 0
    for axis, stride, radix, _ in stages:
        digit = lax.rem(lax.div(spot[axis], stride), radix)
        for k in range(1, radix):
            greet(axis, spot[axis] + (lax.rem(digit + k, radix) - digit) * stride)
            greeted += 1

    apart = all(radix < shards for axis, _, radix, _ in stages if axis == "ctx")
    if apart:

        @pl.when(has_edge)
        def _():
            greet("ctx", edge_peer)

    own_copies, in_copies = [], []
    for c in range(chunks):
        lanes = pl.ds(c * LANES, LANES)
        for which, (part, shared) in enumerate(((k_hbm, gk_hbm), (v_hbm, gv_hbm))):
            own_copies.append(
                pltpu.make_async_copy(
                    part.at[:, lanes], kv.at[c, which, pl.ds(0, rows)], own_sem.at[0, c, which]
                )
            )
            in_copies.append(
                pltpu.make_async_copy(
                    shared.at[:, lanes],
                    kv.at[c, which, pl.ds(glob_at, globals_)],
                    own_sem.at[1, c, which],
                )
            )
    for i, (src, dst) in enumerate(
        ((ps_hbm, ps_ref), (pb_hbm, pb_ref), (q_hbm, q_ref), (u_hbm, u_ref))
    ):
        in_copies.append(pltpu.make_async_copy(src, dst, in_sem.at[i]))
    for copy in own_copies + in_copies:
        copy.start()
    for copy in own_copies:
        copy.wait()

    pl.semaphore_wait(barrier, greeted + jnp.where(has_edge, 1, 0) if apart else greeted)

    def kv_copy(c, b):
        return pltpu.make_async_remote_copy(
            src_ref=kv.at[c, :, pl.ds(0, rows)],
            dst_ref=kv.at[c, :, pl.ds(rows * (1 + b), rows)],
            send_sem=kv_send.at[c, b], recv_sem=kv_recv.at[c, b],
            device_id={"ctx": peers[b]}, device_id_type=MESH,
        )

    def kv_edge(c):
        return pltpu.make_async_remote_copy(
            src_ref=kv.at[c, :, pl.ds(edge_first, BLOCK)],
            dst_ref=kv.at[c, :, pl.ds(edge_at, BLOCK)],
            send_sem=kv_send.at[c, bits], recv_sem=kv_recv.at[c, bits],
            device_id={"ctx": edge_peer}, device_id_type=MESH,
        )

    def term_copy(c, b):
        return pltpu.make_async_remote_copy(
            src_ref=terms.at[c, :, pl.ds(rows * b, rows)],
            dst_ref=back.at[c, :, pl.ds(rows * b, rows)],
            send_sem=t_send.at[c, b], recv_sem=t_recv.at[c, b],
            device_id={"ctx": peers[b]}, device_id_type=MESH,
        )

    def term_edge(c):
        return pltpu.make_async_remote_copy(
            src_ref=terms.at[c, :, pl.ds(rows * bits, BLOCK)],
            dst_ref=back.at[c, :, pl.ds(rows * bits, BLOCK)],
            send_sem=t_send.at[c, bits], recv_sem=t_recv.at[c, bits],
            device_id={"ctx": edge_peer}, device_id_type=MESH,
        )

    order = list(range(bits))[::-1]

    def send_kv(c):
        for b in order:
            kv_copy(c, b).start()

        @pl.when(has_edge)
        def _():
            kv_edge(c).start()

    def send_terms(c):
        for b in order:
            term_copy(c, b).start()

        @pl.when(has_edge)
        def _():
            term_edge(c).start()

    ahead = min(3, chunks)
    for c in range(ahead):
        send_kv(c)

    for copy in in_copies:
        copy.wait()

    @pl.when(jnp.logical_not(has_edge))
    def _():
        kv[:, :, edge_at : edge_at + BLOCK] = jnp.zeros((chunks, 2, BLOCK, LANES), kv.dtype)
        back[:, :, rows * bits : rows * bits + BLOCK] = jnp.zeros(
            (chunks, 2, BLOCK, LANES), back.dtype
        )

    pair = 2 * rows
    query_block = lax.rem(lax.div(lax.broadcasted_iota(jnp.int32, (8, pair), 1), BLOCK), blocks)
    first_block = me * blocks
    listed = [
        [(ps_ref[r, first_block + n], pb_ref[r, first_block + n]) for r in range(R)]
        for n in range(blocks)
    ]

    def put_bias(at, counts):
        times = jnp.zeros((8, pair), jnp.int32)
        for n in range(blocks):
            times = jnp.where(query_block == n, counts[n], times)
        times = times.astype(jnp.float32)
        line = jnp.where(times > 0.5, jnp.log(jnp.maximum(times, 1.0)), MASKED)
        for step in range(BLOCK // 8):
            bias[at + step * 8 : at + step * 8 + 8] = line

    for j in range(blocks):
        put_bias(j * BLOCK, [jnp.int32(1 if abs(j - n) <= 1 else 0) for n in range(blocks)])
    for b in range(bits):
        for j in range(blocks):
            counts = []
            for n in range(blocks):
                times = jnp.int32(0)
                for shard, block in listed[n]:
                    times += jnp.where(shard == peers[b], 1, 0) * jnp.where(block == j, 1, 0)
                if b == 0 and j == 0 and n == blocks - 1:
                    times += 1 - odd
                if b == 0 and j == blocks - 1 and n == 0:
                    times += odd
                counts.append(times)
            put_bias(rows * (1 + b) + j * BLOCK, counts)
    valid = jnp.where(has_edge, 1, 0)
    edge_counts = [jnp.int32(0)] * blocks
    edge_counts[0] = edge_counts[0] + (1 - odd) * valid
    edge_counts[blocks - 1] = edge_counts[blocks - 1] + odd * valid
    put_bias(edge_at, edge_counts)
    for at in range(glob_at, glob_at + globals_, BLOCK):
        put_bias(at, [jnp.int32(1)] * blocks)

    low_head = lax.broadcasted_iota(jnp.int32, (rows, LANES), 1) < HEAD_DIM
    scaling = 1.0 / math.sqrt(HEAD_DIM)

    def both_heads(x):
        x = x.astype(jnp.float32)
        zero = jnp.zeros_like(x)
        return jnp.concatenate(
            [jnp.where(low_head, x, zero), jnp.where(low_head, zero, x)], axis=0
        )

    def dot(a, b, dims):
        return lax.dot_general(a, b, dims, preferred_element_type=jnp.float32)

    NN = (((1,), (0,)), ((), ()))

    def by_query(x):
        return jnp.concatenate([x[:HEAD_DIM, :rows], x[HEAD_DIM:, rows:]], axis=0).T

    def digit_of(i):
        axis, stride, radix, _ = stages[i]
        return lax.rem(lax.div(spot[axis], stride), radix)

    def peer_of(i, k):
        axis, stride, radix, _ = stages[i]
        digit = digit_of(i)
        other = lax.rem(digit + k, radix)
        return other, {axis: spot[axis] + (other - digit) * stride}

    def scatter_copy(i, k):
        held = stages[i][3]
        other, device = peer_of(i, k)
        at = other * held if accs[i].shape[0] != held else 0
        return pltpu.make_async_remote_copy(
            src_ref=accs[i].at[pl.ds(pl.multiple_of(at, 16), held)],
            dst_ref=recvs[i].at[k - 1],
            send_sem=rs_send[i].at[k - 1], recv_sem=rs_recv[i].at[k - 1],
            device_id=device, device_id_type=MESH,
        )

    def step(c, carry):
        lanes = pl.ds(pl.multiple_of(c * LANES, LANES), LANES)
        queries = (both_heads(q_ref[:, lanes]) * scaling).astype(jnp.bfloat16)
        grads = both_heads(u_ref[:, lanes]).astype(jnp.bfloat16)
        for b in order:
            kv_copy(c, b).wait_recv()

        @pl.when(has_edge)
        def _():
            kv_edge(c).wait_recv()

        @pl.when(c + ahead < chunks)
        def _():
            send_kv(c + ahead)

        top = None
        for at, size in tiles:
            rows_at = slice(at, at + size)
            scores = dot(kv[c, 0, rows_at], queries, NT) + bias[rows_at]
            weight_s[rows_at] = scores
            part = jnp.max(scores, axis=0, keepdims=True)
            top = part if top is None else jnp.maximum(top, part)
        norm = mixed = jnp.zeros((1, pair), jnp.float32)
        for at, size in tiles:
            rows_at = slice(at, at + size)
            weights = jnp.exp(weight_s[rows_at] - top)
            dprobs = dot(kv[c, 1, rows_at], grads, NT)
            weight_s[rows_at] = weights
            dprob_s[rows_at] = dprobs
            norm = norm + jnp.sum(weights, axis=0, keepdims=True)
            mixed = mixed + jnp.sum(weights * dprobs, axis=0, keepdims=True)
        inverse = 1.0 / norm
        inner = mixed * inverse

        def products(at, size):
            rows_at = slice(at, at + size)
            probs = weight_s[rows_at] * inverse
            low = probs.astype(jnp.bfloat16)
            dscores = (probs * (dprob_s[rows_at] - inner)).astype(jnp.bfloat16)
            low_s[rows_at] = low
            dscore_s[rows_at] = dscores
            return dot(dscores, queries, NN), dot(low, grads, NN)

        for which, made in enumerate(products(*tiles[-1])):
            accs[0][
                pl.ds(pl.multiple_of((c * 2 + which) * globals_, globals_), globals_)
            ] = made.astype(jnp.bfloat16)
        for k in range(1, stages[0][2]):
            held = stages[0][3]
            ready = lax.div((peer_of(0, k)[0] + 1) * held - 1, 2 * globals_)
            if accs[0].shape[0] == held:
                ready = chunks - 1

            @pl.when(c == ready)
            def _(k=k):
                scatter_copy(0, k).start()

        for at, size in tiles[1:-1]:
            for which, made in enumerate(products(at, size)):
                terms[c, which, at - rows : at - rows + size] = made.astype(jnp.bfloat16)

        @pl.when(c < chunks - 1)
        def _():
            send_terms(c)

        for which, made in enumerate(products(*tiles[0])):
            own[c, which] = made
        att_ref[:, lanes] = by_query(dot(kv[c, 1], low_s[...], TN)).astype(jnp.bfloat16)
        dq_ref[:, lanes] = (by_query(dot(kv[c, 0], dscore_s[...], TN)) * scaling).astype(
            jnp.bfloat16
        )
        return carry

    lax.fori_loop(0, chunks, step, 0)
    out_copies = [
        pltpu.make_async_copy(ref, out, out_sem.at[i])
        for i, (ref, out) in enumerate(
            zip((att_ref, dq_ref, dk_ref, dv_ref, dgk_ref, dgv_ref), outs_hbm)
        )
    ]
    out_copies[0].start()
    out_copies[1].start()

    starts = []
    start = 0
    for i, (axis, stride, radix, held) in enumerate(stages):
        if accs[i].shape[0] != held:
            start = start + digit_of(i) * held
        starts.append(start)

    def scatter_start(i):
        for k in range(1, stages[i][2]):
            scatter_copy(i, k).start()

    def scatter_end(i):
        held = stages[i][3]
        at = digit_of(i) * held if accs[i].shape[0] != held else 0
        summed = accs[i][pl.ds(pl.multiple_of(at, 16), held)].astype(jnp.float32)
        for k in range(1, stages[i][2]):
            scatter_copy(i, k).wait_recv()
            summed = summed + recvs[i][k - 1].astype(jnp.float32)
        summed = summed.astype(jnp.bfloat16)
        if i + 1 < count:
            accs[i + 1][...] = summed
        else:
            final[pl.ds(pl.multiple_of(starts[i], 16), held)] = summed

    def gather_copy(i, k, at):
        held = stages[i][3]
        part = final.at[pl.ds(pl.multiple_of(at, 16), held)]
        return pltpu.make_async_remote_copy(
            src_ref=part, dst_ref=part,
            send_sem=ag_send[i].at[k - 1], recv_sem=ag_recv[i].at[k - 1],
            device_id=peer_of(i, k)[1], device_id_type=MESH,
        )

    def gather_start(i):
        for k in range(1, stages[i][2]):
            gather_copy(i, k, starts[i]).start()

    def gather_end(i):
        _, _, radix, held = stages[i]
        for k in range(1, radix):
            behind = lax.rem(digit_of(i) + radix - k, radix)
            gather_copy(i, k, starts[i] + (behind - digit_of(i)) * held).wait_recv()

    def collect(c):
        lanes = slice(c * LANES, (c + 1) * LANES)
        for b in order:
            term_copy(c, b).wait_recv()

        @pl.when(has_edge)
        def _():
            term_edge(c).wait_recv()

        low_rows = lax.broadcasted_iota(jnp.int32, (rows, LANES), 0)
        at_edge = jnp.logical_and(low_rows >= edge_first, low_rows < edge_first + BLOCK)
        for which, out in enumerate((dk_ref, dv_ref)):
            summed = own[c, which]
            for b in range(bits):
                summed = summed + back[c, which, rows * b : rows * (b + 1)].astype(jnp.float32)
            edge = back[c, which, rows * bits : rows * bits + BLOCK].astype(jnp.float32)
            edge = jnp.concatenate([edge] * blocks, axis=0)
            summed = summed + jnp.where(at_edge, edge, 0.0)
            out[:, lanes] = summed.astype(jnp.bfloat16)

    todo = list(range(chunks))
    for i in range(count):
        if i:
            scatter_start(i)
        scatter_end(i)
    split = [i for i in range(count) if accs[i].shape[0] != stages[i][3]]
    for i in split[::-1]:
        gather_start(i)
        if i == split[-1]:
            send_terms(chunks - 1)
        if len(todo) > 1:
            collect(todo.pop(0))
        gather_end(i)
    for c in range(chunks):
        lanes = slice(c * LANES, (c + 1) * LANES)
        for which, out in enumerate((dgk_ref, dgv_ref)):
            at = (c * 2 + which) * globals_
            out[:, lanes] = final[at : at + globals_].astype(jnp.float32)
    out_copies[4].start()
    out_copies[5].start()
    for c in todo:
        collect(c)
    out_copies[2].start()
    out_copies[3].start()

    for c in range(chunks):
        for b in order:
            kv_copy(c, b).wait_send()
            term_copy(c, b).wait_send()

        @pl.when(has_edge)
        def _():
            kv_edge(c).wait_send()
            term_edge(c).wait_send()

    for i in range(count):
        for k in range(1, stages[i][2]):
            scatter_copy(i, k).wait_send()
            if i in split:
                gather_copy(i, k, starts[i]).wait_send()

    for copy in out_copies:
        copy.wait()


def write_out(*refs):
    count = len(refs) // 3
    sem = refs[-1]
    loads = [
        pltpu.make_async_copy(refs[i], refs[2 * count + i], sem.at[0, i]) for i in range(count)
    ]
    stores = [
        pltpu.make_async_copy(refs[2 * count + i], refs[count + i], sem.at[1, i])
        for i in range(count)
    ]
    for copy in loads:
        copy.start()
    for load, store in zip(loads, stores):
        load.wait()
        store.start()
    for copy in stores:
        copy.wait()


def body(shards, replicas, queries, keys, values, global_keys, global_values, upstream, ps, pb):
    _, rows, width = queries.shape
    globals_ = global_keys.shape[0]
    bits = shards.bit_length() - 1
    chunks = width // LANES
    total = rows * (1 + bits) + BLOCK + globals_
    gathered = 2 * chunks * globals_
    stages = reduce_stages((("dp", replicas), ("ctx", shards)), gathered)
    low = jnp.bfloat16
    accs, recvs, sems = [], [], []
    held = gathered
    for _, _, radix, after in stages:
        accs.append(pltpu.VMEM((held, LANES), low))
        recvs.append(pltpu.VMEM((radix - 1, after, LANES), low))
        sems.append(pltpu.SemaphoreType.DMA((radix - 1,)))
        held = after
    hbm = pl.BlockSpec(memory_space=pltpu.HBM)
    dma = pltpu.SemaphoreType.DMA((chunks, bits + 1))
    remote = rows * bits + BLOCK
    results = [((rows, width), low)] * 4 + [((globals_, width), jnp.float32)] * 2
    outs = pl.pallas_call(
        functools.partial(kernel, shards, stages),
        out_shape=[jax.ShapeDtypeStruct(*x) for x in results],
        in_specs=[hbm] * 8,
        out_specs=[hbm] * 6,
        scratch_shapes=[
            *[pltpu.VMEM(*x) for x in results],
            pltpu.SemaphoreType.DMA((6,)),
            pltpu.VMEM((rows, width), low),
            pltpu.VMEM((rows, width), low),
            pltpu.SMEM(ps.T.shape, jnp.int32),
            pltpu.SMEM(pb.T.shape, jnp.int32),
            pltpu.SemaphoreType.DMA((4,)),
            pltpu.SemaphoreType.DMA((2, chunks, 2)),
            *[pltpu.VMEM((total, 2 * rows), x) for x in (jnp.float32, jnp.float32, low, low)],
            pltpu.VMEM((chunks, 2, total, LANES), low),
            pltpu.VMEM((total, 2 * rows), jnp.float32),
            pltpu.VMEM((chunks, 2, remote, LANES), low),
            pltpu.VMEM((chunks, 2, remote, LANES), low),
            pltpu.VMEM((chunks, 2, rows, LANES), jnp.float32),
            *accs,
            *recvs,
            pltpu.VMEM((gathered, LANES), low),
            dma, dma, dma, dma,
            *sems, *sems, *sems, *sems,
        ],
        compiler_params=pltpu.CompilerParams(
            collective_id=0, has_side_effects=True, vmem_limit_bytes=VMEM_BYTES
        ),
    )(queries[0], keys[0], values[0], global_keys, global_values, upstream[0], ps.T, pb.T)
    outs = pl.pallas_call(
        write_out,
        out_shape=[jax.ShapeDtypeStruct(x.shape, x.dtype) for x in outs],
        in_specs=[hbm] * 6,
        out_specs=[hbm] * 6,
        scratch_shapes=[
            *[pltpu.VMEM(*x) for x in results],
            pltpu.SemaphoreType.DMA((2, 6)),
        ],
        compiler_params=pltpu.CompilerParams(vmem_limit_bytes=VMEM_BYTES),
    )(*outs)
    return (outs[0][None], outs[1][None], outs[2][None], outs[3][None], outs[4], outs[5])


def solution(mesh):
    split = P("dp", "ctx", None)
    return jax.shard_map(
        functools.partial(body, mesh.shape["ctx"], mesh.shape["dp"]),
        mesh=mesh,
        in_specs=(split, split, split, P(), P(), split, P(), P()),
        out_specs=(split, split, split, split, P(), P()),
        check_vma=False,
    )
```

```python
import functools
import math

import jax
import jax.numpy as jnp
from jax import lax
from jax.experimental import pallas as pl
from jax.experimental.pallas import tpu as pltpu
from jax.sharding import PartitionSpec as P

HEAD_DIM = 64
BLOCK = 64
R = 3
LANES = 128
VMEM_BYTES = 63 * 1024 * 1024
MASKED = -1e30
MESH = pl.DeviceIdType.MESH
NT = (((1,), (1,)), ((), ()))
TN = (((0,), (0,)), ((), ()))


def reduce_stages(sizes, rows):
    stages = []
    for axis, size in sizes:
        stride = 1
        while stride < size:
            radix = min(2 if axis == "ctx" and stride == 1 else 8, size // stride)
            if rows % (radix * 16) == 0:
                rows //= radix
            stages.append((axis, stride, radix, rows))
            stride *= radix
    return stages


def kernel(
    shards, stages, q_hbm, k_hbm, v_hbm, gk_hbm, gv_hbm, u_hbm, ps_hbm, pb_hbm,
    *refs,
):
    outs_hbm, (att_ref, dq_ref, dk_ref, dv_ref, dgk_ref, dgv_ref) = refs[:6], refs[6:12]
    run(
        shards, stages, q_hbm, k_hbm, v_hbm, gk_hbm, gv_hbm, u_hbm, ps_hbm, pb_hbm, outs_hbm,
        att_ref, dq_ref, dk_ref, dv_ref, dgk_ref, dgv_ref, *refs[12:],
    )


def run(
    shards, stages, q_hbm, k_hbm, v_hbm, gk_hbm, gv_hbm, u_hbm, ps_hbm, pb_hbm, outs_hbm,
    att_ref, dq_ref, dk_ref, dv_ref, dgk_ref, dgv_ref, out_sem,
    q_ref, u_ref, ps_ref, pb_ref, in_sem, own_sem, weight_s, dprob_s, low_s, dscore_s, kv, bias, terms, back, own, *rest,
):
    count = len(stages)
    accs, recvs = rest[:count], rest[count : 2 * count]
    final = rest[2 * count]
    kv_send, kv_recv, t_send, t_recv = rest[2 * count + 1 : 2 * count + 5]
    sems = rest[2 * count + 5 :]
    rs_send, rs_recv = sems[:count], sems[count : 2 * count]
    ag_send, ag_recv = sems[2 * count : 3 * count], sems[3 * count :]

    rows, width = q_hbm.shape
    blocks = rows // BLOCK
    chunks = width // LANES
    bits = shards.bit_length() - 1
    globals_ = gk_hbm.shape[0]
    edge_at = rows * (1 + bits)
    glob_at = edge_at + BLOCK
    tiles = [(rows * i, rows) for i in range(1 + bits)] + [(edge_at, BLOCK), (glob_at, globals_)]
    me = lax.axis_index("ctx")
    spot = {"ctx": me, "dp": lax.axis_index("dp")}
    odd = lax.rem(me, 2)
    edge_peer = me - 1 + 2 * odd
    has_edge = jnp.logical_and(edge_peer >= 0, edge_peer < shards)
    edge_first = pl.multiple_of(odd * (rows - BLOCK), BLOCK)
    peers = [me + (1 << b) * (1 - 2 * lax.rem(lax.div(me, 1 << b), 2)) for b in range(bits)]

    barrier = pltpu.get_barrier_semaphore()

    def greet(axis, to):
        pl.semaphore_signal(barrier, inc=1, device_id={axis: to}, device_id_type=MESH)

    greeted = 0
    for axis, stride, radix, _ in stages:
        digit = lax.rem(lax.div(spot[axis], stride), radix)
        for k in range(1, radix):
            greet(axis, spot[axis] + (lax.rem(digit + k, radix) - digit) * stride)
            greeted += 1

    apart = all(radix < shards for axis, _, radix, _ in stages if axis == "ctx")
    if apart:

        @pl.when(has_edge)
        def _():
            greet("ctx", edge_peer)

    own_copies, in_copies = [], []
    for c in range(chunks):
        lanes = pl.ds(c * LANES, LANES)
        for which, (part, shared) in enumerate(((k_hbm, gk_hbm), (v_hbm, gv_hbm))):
            own_copies.append(
                pltpu.make_async_copy(
                    part.at[:, lanes], kv.at[c, which, pl.ds(0, rows)], own_sem.at[0, c, which]
                )
            )
            in_copies.append(
                pltpu.make_async_copy(
                    shared.at[:, lanes],
                    kv.at[c, which, pl.ds(glob_at, globals_)],
                    own_sem.at[1, c, which],
                )
            )
    for i, (src, dst) in enumerate(
        ((ps_hbm, ps_ref), (pb_hbm, pb_ref), (q_hbm, q_ref), (u_hbm, u_ref))
    ):
        in_copies.append(pltpu.make_async_copy(src, dst, in_sem.at[i]))
    for copy in own_copies + in_copies:
        copy.start()
    for copy in own_copies:
        copy.wait()

    pl.semaphore_wait(barrier, greeted + jnp.where(has_edge, 1, 0) if apart else greeted)

    def kv_copy(c, b):
        return pltpu.make_async_remote_copy(
            src_ref=kv.at[c, :, pl.ds(0, rows)],
            dst_ref=kv.at[c, :, pl.ds(rows * (1 + b), rows)],
            send_sem=kv_send.at[c, b], recv_sem=kv_recv.at[c, b],
            device_id={"ctx": peers[b]}, device_id_type=MESH,
        )

    def kv_edge(c):
        return pltpu.make_async_remote_copy(
            src_ref=kv.at[c, :, pl.ds(edge_first, BLOCK)],
            dst_ref=kv.at[c, :, pl.ds(edge_at, BLOCK)],
            send_sem=kv_send.at[c, bits], recv_sem=kv_recv.at[c, bits],
            device_id={"ctx": edge_peer}, device_id_type=MESH,
        )

    def term_copy(c, b):
        return pltpu.make_async_remote_copy(
            src_ref=terms.at[c, :, pl.ds(rows * b, rows)],
            dst_ref=back.at[c, :, pl.ds(rows * b, rows)],
            send_sem=t_send.at[c, b], recv_sem=t_recv.at[c, b],
            device_id={"ctx": peers[b]}, device_id_type=MESH,
        )

    def term_edge(c):
        return pltpu.make_async_remote_copy(
            src_ref=terms.at[c, :, pl.ds(rows * bits, BLOCK)],
            dst_ref=back.at[c, :, pl.ds(rows * bits, BLOCK)],
            send_sem=t_send.at[c, bits], recv_sem=t_recv.at[c, bits],
            device_id={"ctx": edge_peer}, device_id_type=MESH,
        )

    order = list(range(bits))[::-1]

    def send_kv(c):
        for b in order:
            kv_copy(c, b).start()

        @pl.when(has_edge)
        def _():
            kv_edge(c).start()

    def send_terms(c):
        for b in order:
            term_copy(c, b).start()

        @pl.when(has_edge)
        def _():
            term_edge(c).start()

    ahead = min(2, chunks)
    for c in range(ahead):
        send_kv(c)

    for copy in in_copies:
        copy.wait()

    @pl.when(jnp.logical_not(has_edge))
    def _():
        kv[:, :, edge_at : edge_at + BLOCK] = jnp.zeros((chunks, 2, BLOCK, LANES), kv.dtype)
        back[:, :, rows * bits : rows * bits + BLOCK] = jnp.zeros(
            (chunks, 2, BLOCK, LANES), back.dtype
        )

    pair = 2 * rows
    query_block = lax.rem(lax.div(lax.broadcasted_iota(jnp.int32, (8, pair), 1), BLOCK), blocks)
    first_block = me * blocks
    listed = [
        [(ps_ref[r, first_block + n], pb_ref[r, first_block + n]) for r in range(R)]
        for n in range(blocks)
    ]

    def put_bias(at, counts):
        times = jnp.zeros((8, pair), jnp.int32)
        for n in range(blocks):
            times = jnp.where(query_block == n, counts[n], times)
        times = times.astype(jnp.float32)
        line = jnp.where(times > 0.5, jnp.log(jnp.maximum(times, 1.0)), MASKED)
        for step in range(BLOCK // 8):
            bias[at + step * 8 : at + step * 8 + 8] = line

    for j in range(blocks):
        put_bias(j * BLOCK, [jnp.int32(1 if abs(j - n) <= 1 else 0) for n in range(blocks)])
    for b in range(bits):
        for j in range(blocks):
            counts = []
            for n in range(blocks):
                times = jnp.int32(0)
                for shard, block in listed[n]:
                    times += jnp.where(shard == peers[b], 1, 0) * jnp.where(block == j, 1, 0)
                if b == 0 and j == 0 and n == blocks - 1:
                    times += 1 - odd
                if b == 0 and j == blocks - 1 and n == 0:
                    times += odd
                counts.append(times)
            put_bias(rows * (1 + b) + j * BLOCK, counts)
    valid = jnp.where(has_edge, 1, 0)
    edge_counts = [jnp.int32(0)] * blocks
    edge_counts[0] = edge_counts[0] + (1 - odd) * valid
    edge_counts[blocks - 1] = edge_counts[blocks - 1] + odd * valid
    put_bias(edge_at, edge_counts)
    for at in range(glob_at, glob_at + globals_, BLOCK):
        put_bias(at, [jnp.int32(1)] * blocks)

    low_head = lax.broadcasted_iota(jnp.int32, (rows, LANES), 1) < HEAD_DIM
    scaling = 1.0 / math.sqrt(HEAD_DIM)

    def both_heads(x):
        x = x.astype(jnp.float32)
        zero = jnp.zeros_like(x)
        return jnp.concatenate(
            [jnp.where(low_head, x, zero), jnp.where(low_head, zero, x)], axis=0
        )

    def dot(a, b, dims):
        return lax.dot_general(a, b, dims, preferred_element_type=jnp.float32)

    NN = (((1,), (0,)), ((), ()))

    def by_query(x):
        return jnp.concatenate([x[:HEAD_DIM, :rows], x[HEAD_DIM:, rows:]], axis=0).T

    def digit_of(i):
        axis, stride, radix, _ = stages[i]
        return lax.rem(lax.div(spot[axis], stride), radix)

    def peer_of(i, k):
        axis, stride, radix, _ = stages[i]
        digit = digit_of(i)
        other = lax.rem(digit + k, radix)
        return other, {axis: spot[axis] + (other - digit) * stride}

    def scatter_copy(i, k):
        held = stages[i][3]
        other, device = peer_of(i, k)
        at = other * held if accs[i].shape[0] != held else 0
        return pltpu.make_async_remote_copy(
            src_ref=accs[i].at[pl.ds(pl.multiple_of(at, 16), held)],
            dst_ref=recvs[i].at[k - 1],
            send_sem=rs_send[i].at[k - 1], recv_sem=rs_recv[i].at[k - 1],
            device_id=device, device_id_type=MESH,
        )

    def step(c, carry):
        lanes = pl.ds(pl.multiple_of(c * LANES, LANES), LANES)
        queries = (both_heads(q_ref[:, lanes]) * scaling).astype(jnp.bfloat16)
        grads = both_heads(u_ref[:, lanes]).astype(jnp.bfloat16)
        for b in order:
            kv_copy(c, b).wait_recv()

        @pl.when(has_edge)
        def _():
            kv_edge(c).wait_recv()

        @pl.when(c + ahead < chunks)
        def _():
            send_kv(c + ahead)

        @pl.when(c == chunks - 1)
        def _():
            for done in range(chunks - 2):
                send_terms(done)

        top = None
        for at, size in tiles:
            rows_at = slice(at, at + size)
            scores = dot(kv[c, 0, rows_at], queries, NT) + bias[rows_at]
            weight_s[rows_at] = scores
            part = jnp.max(scores, axis=0, keepdims=True)
            top = part if top is None else jnp.maximum(top, part)
        norm = mixed = jnp.zeros((1, pair), jnp.float32)
        for at, size in tiles:
            rows_at = slice(at, at + size)
            weights = jnp.exp(weight_s[rows_at] - top)
            dprobs = dot(kv[c, 1, rows_at], grads, NT)
            weight_s[rows_at] = weights
            dprob_s[rows_at] = dprobs
            norm = norm + jnp.sum(weights, axis=0, keepdims=True)
            mixed = mixed + jnp.sum(weights * dprobs, axis=0, keepdims=True)
        inverse = 1.0 / norm
        inner = mixed * inverse

        def products(at, size):
            rows_at = slice(at, at + size)
            probs = weight_s[rows_at] * inverse
            low = probs.astype(jnp.bfloat16)
            dscores = (probs * (dprob_s[rows_at] - inner)).astype(jnp.bfloat16)
            low_s[rows_at] = low
            dscore_s[rows_at] = dscores
            return dot(dscores, queries, NN), dot(low, grads, NN)

        for which, made in enumerate(products(*tiles[-1])):
            accs[0][
                pl.ds(pl.multiple_of((c * 2 + which) * globals_, globals_), globals_)
            ] = made.astype(jnp.bfloat16)
        for k in range(1, stages[0][2]):
            held = stages[0][3]
            ready = lax.div((peer_of(0, k)[0] + 1) * held - 1, 2 * globals_)
            if accs[0].shape[0] == held:
                ready = chunks - 1

            @pl.when(c == ready)
            def _(k=k):
                scatter_copy(0, k).start()

        for at, size in tiles[1:-1]:
            for which, made in enumerate(products(at, size)):
                terms[c, which, at - rows : at - rows + size] = made.astype(jnp.bfloat16)
        for which, made in enumerate(products(*tiles[0])):
            own[c, which] = made
        att_ref[:, lanes] = by_query(dot(kv[c, 1], low_s[...], TN)).astype(jnp.bfloat16)
        dq_ref[:, lanes] = (by_query(dot(kv[c, 0], dscore_s[...], TN)) * scaling).astype(
            jnp.bfloat16
        )
        return carry

    lax.fori_loop(0, chunks, step, 0)
    out_copies = [
        pltpu.make_async_copy(ref, out, out_sem.at[i])
        for i, (ref, out) in enumerate(
            zip((att_ref, dq_ref, dk_ref, dv_ref, dgk_ref, dgv_ref), outs_hbm)
        )
    ]
    out_copies[0].start()
    out_copies[1].start()

    starts = []
    start = 0
    for i, (axis, stride, radix, held) in enumerate(stages):
        if accs[i].shape[0] != held:
            start = start + digit_of(i) * held
        starts.append(start)

    def scatter_start(i):
        for k in range(1, stages[i][2]):
            scatter_copy(i, k).start()

    def scatter_end(i):
        held = stages[i][3]
        at = digit_of(i) * held if accs[i].shape[0] != held else 0
        summed = accs[i][pl.ds(pl.multiple_of(at, 16), held)].astype(jnp.float32)
        for k in range(1, stages[i][2]):
            scatter_copy(i, k).wait_recv()
            summed = summed + recvs[i][k - 1].astype(jnp.float32)
        summed = summed.astype(jnp.bfloat16)
        if i + 1 < count:
            accs[i + 1][...] = summed
        else:
            final[pl.ds(pl.multiple_of(starts[i], 16), held)] = summed

    def gather_copy(i, k, at):
        held = stages[i][3]
        part = final.at[pl.ds(pl.multiple_of(at, 16), held)]
        return pltpu.make_async_remote_copy(
            src_ref=part, dst_ref=part,
            send_sem=ag_send[i].at[k - 1], recv_sem=ag_recv[i].at[k - 1],
            device_id=peer_of(i, k)[1], device_id_type=MESH,
        )

    def gather_start(i):
        for k in range(1, stages[i][2]):
            gather_copy(i, k, starts[i]).start()

    def gather_end(i):
        _, _, radix, held = stages[i]
        for k in range(1, radix):
            behind = lax.rem(digit_of(i) + radix - k, radix)
            gather_copy(i, k, starts[i] + (behind - digit_of(i)) * held).wait_recv()

    def collect(c):
        lanes = slice(c * LANES, (c + 1) * LANES)
        for b in order:
            term_copy(c, b).wait_recv()

        @pl.when(has_edge)
        def _():
            term_edge(c).wait_recv()

        low_rows = lax.broadcasted_iota(jnp.int32, (rows, LANES), 0)
        at_edge = jnp.logical_and(low_rows >= edge_first, low_rows < edge_first + BLOCK)
        for which, out in enumerate((dk_ref, dv_ref)):
            summed = own[c, which]
            for b in range(bits):
                summed = summed + back[c, which, rows * b : rows * (b + 1)].astype(jnp.float32)
            edge = back[c, which, rows * bits : rows * bits + BLOCK].astype(jnp.float32)
            edge = jnp.concatenate([edge] * blocks, axis=0)
            summed = summed + jnp.where(at_edge, edge, 0.0)
            out[:, lanes] = summed.astype(jnp.bfloat16)

    todo = list(range(chunks))
    for i in range(count):
        if i:
            scatter_start(i)
        if i == count - 1 and chunks > 1:
            send_terms(chunks - 2)
        scatter_end(i)
    split = [i for i in range(count) if accs[i].shape[0] != stages[i][3]]
    for i in split[::-1]:
        gather_start(i)
        if i == split[-1]:
            send_terms(chunks - 1)
        if len(todo) > 1:
            collect(todo.pop(0))
        gather_end(i)
    for c in range(chunks):
        lanes = slice(c * LANES, (c + 1) * LANES)
        for which, out in enumerate((dgk_ref, dgv_ref)):
            at = (c * 2 + which) * globals_
            out[:, lanes] = final[at : at + globals_].astype(jnp.float32)
    out_copies[4].start()
    out_copies[5].start()
    for c in todo:
        collect(c)
    out_copies[2].start()
    out_copies[3].start()

    for c in range(chunks):
        for b in order:
            kv_copy(c, b).wait_send()
            term_copy(c, b).wait_send()

        @pl.when(has_edge)
        def _():
            kv_edge(c).wait_send()
            term_edge(c).wait_send()

    for i in range(count):
        for k in range(1, stages[i][2]):
            scatter_copy(i, k).wait_send()
            if i in split:
                gather_copy(i, k, starts[i]).wait_send()

    for copy in out_copies:
        copy.wait()


def write_out(*refs):
    count = len(refs) // 3
    sem = refs[-1]
    loads = [
        pltpu.make_async_copy(refs[i], refs[2 * count + i], sem.at[0, i]) for i in range(count)
    ]
    stores = [
        pltpu.make_async_copy(refs[2 * count + i], refs[count + i], sem.at[1, i])
        for i in range(count)
    ]
    for copy in loads:
        copy.start()
    for load, store in zip(loads, stores):
        load.wait()
        store.start()
    for copy in stores:
        copy.wait()


def body(shards, replicas, queries, keys, values, global_keys, global_values, upstream, ps, pb):
    _, rows, width = queries.shape
    globals_ = global_keys.shape[0]
    bits = shards.bit_length() - 1
    chunks = width // LANES
    total = rows * (1 + bits) + BLOCK + globals_
    gathered = 2 * chunks * globals_
    stages = reduce_stages((("dp", replicas), ("ctx", shards)), gathered)
    low = jnp.bfloat16
    accs, recvs, sems = [], [], []
    held = gathered
    for _, _, radix, after in stages:
        accs.append(pltpu.VMEM((held, LANES), low))
        recvs.append(pltpu.VMEM((radix - 1, after, LANES), low))
        sems.append(pltpu.SemaphoreType.DMA((radix - 1,)))
        held = after
    hbm = pl.BlockSpec(memory_space=pltpu.HBM)
    dma = pltpu.SemaphoreType.DMA((chunks, bits + 1))
    remote = rows * bits + BLOCK
    results = [((rows, width), low)] * 4 + [((globals_, width), jnp.float32)] * 2
    outs = pl.pallas_call(
        functools.partial(kernel, shards, stages),
        out_shape=[jax.ShapeDtypeStruct(*x) for x in results],
        in_specs=[hbm] * 8,
        out_specs=[hbm] * 6,
        scratch_shapes=[
            *[pltpu.VMEM(*x) for x in results],
            pltpu.SemaphoreType.DMA((6,)),
            pltpu.VMEM((rows, width), low),
            pltpu.VMEM((rows, width), low),
            pltpu.SMEM(ps.T.shape, jnp.int32),
            pltpu.SMEM(pb.T.shape, jnp.int32),
            pltpu.SemaphoreType.DMA((4,)),
            pltpu.SemaphoreType.DMA((2, chunks, 2)),
            *[pltpu.VMEM((total, 2 * rows), x) for x in (jnp.float32, jnp.float32, low, low)],
            pltpu.VMEM((chunks, 2, total, LANES), low),
            pltpu.VMEM((total, 2 * rows), jnp.float32),
            pltpu.VMEM((chunks, 2, remote, LANES), low),
            pltpu.VMEM((chunks, 2, remote, LANES), low),
            pltpu.VMEM((chunks, 2, rows, LANES), jnp.float32),
            *accs,
            *recvs,
            pltpu.VMEM((gathered, LANES), low),
            dma, dma, dma, dma,
            *sems, *sems, *sems, *sems,
        ],
        compiler_params=pltpu.CompilerParams(
            collective_id=0, has_side_effects=True, vmem_limit_bytes=VMEM_BYTES
        ),
    )(queries[0], keys[0], values[0], global_keys, global_values, upstream[0], ps.T, pb.T)
    outs = pl.pallas_call(
        write_out,
        out_shape=[jax.ShapeDtypeStruct(x.shape, x.dtype) for x in outs],
        in_specs=[hbm] * 6,
        out_specs=[hbm] * 6,
        scratch_shapes=[
            *[pltpu.VMEM(*x) for x in results],
            pltpu.SemaphoreType.DMA((2, 6)),
        ],
        compiler_params=pltpu.CompilerParams(vmem_limit_bytes=VMEM_BYTES),
    )(*outs)
    return (outs[0][None], outs[1][None], outs[2][None], outs[3][None], outs[4], outs[5])


def solution(mesh):
    split = P("dp", "ctx", None)
    return jax.shard_map(
        functools.partial(body, mesh.shape["ctx"], mesh.shape["dp"]),
        mesh=mesh,
        in_specs=(split, split, split, P(), P(), split, P(), P()),
        out_specs=(split, split, split, split, P(), P()),
        check_vma=False,
    )
```
